256 devices in a mesh: strike: 16 (over z, core), dip: 4 (over x), depth: 4 (over y).
Axes of the slice: x: 4, y: 4, z: 8, core: 2. Of those that a mesh axis runs over, the one named last changes fastest.
Arguments:
- state: float32 [20, 27, 131072], P(None, None, ('strike', 'dip', 'depth')), may hold values from -6 to 6
- geometry: float32 [3, 3, 131072], P(None, None, ('strike', 'dip', 'depth')), may hold values from -3 to 3
- normals: float32 [4, 3, 131072], P(None, None, ('strike', 'dip', 'depth')), may hold values from -3 to 3
- wave_speed: float32 [131072], P(('strike', 'dip', 'depth')), may hold values from 0.5 to 2
- cluster: int32 [131072], P(('strike', 'dip', 'depth')), may hold values 0 or 1
- nb_index: int32 [4, 131072], P(None, ('strike', 'dip', 'depth')), may hold values from 0 to 1535, as said below
- nb_face: int32 [4, 131072], P(None, ('strike', 'dip', 'depth')), may hold values from 0 to 3, as said below
- orientation: int32 [4, 131072], P(None, ('strike', 'dip', 'depth')), may hold values from 0 to 2
- export_strike: int32 [2, 65536], P(None, ('strike', 'dip', 'depth')), may hold values from 0 to 2047, as said below
- export_dip: int32 [2, 32768], P(None, ('strike', 'dip', 'depth')), may hold values from 0 to 2047, as said below
- export_depth: int32 [2, 32768], P(None, ('strike', 'dip', 'depth')), may hold values from 0 to 2047, as said below
- stiffness: float32 [3, 20, 20], replicated, may hold values from -1.25 to 1.25
- stiff_volume: float32 [3, 20, 20], replicated, may hold values from -1.25 to 1.25
- jacobians: float32 [3, 27, 27], replicated, may hold values from -0.625 to 0.625
- face_proj: float32 [4, 10, 20], replicated, may hold values from -1.25 to 1.25
- face_lift: float32 [4, 20, 10], replicated, may hold values from -1 to 1
- rotations: float32 [3, 10, 10], replicated, may hold values from -2 to 2
Outputs:
- new_state: float32 [20, 27, 131072], P(None, None, ('strike', 'dip', 'depth'))
The draws below stay inside these ranges and needn't reach their ends.
Inputs may be any that keep to these rules, and one draw needn't show every extreme that they name: `nb_index`: each face is paired with exactly one face: values below 512 name a local element, larger ones a row of the received face blocks as the steps order them; every used row belongs to a linked face, and the link counts reach 256 and 128. `nb_face`: the neighbour's face number of the pairing in nb_index. `export_strike`: entry l names the local face slot of link l to that neighbour; slots beyond a link count hold 0 and are never referred to; some device uses all 256. `export_dip`: as export_strike, with at most 128 links a neighbour. `export_depth`: as export_strike, with at most 128 links a neighbour.
All inputs are finite; a program needn't handle non-finite values. No bound on the sum of `cluster` on one device may be relied on, other than what follows from the above.
Results may differ from the reference program's by a relative error of at most 0.0003.
Values sent between devices are 32-bit elements; how exact they have to be, the bound alone decides.
A program may use at most 128 MiB of HBM per device.

```python
import math
import jax
import jax.numpy as jnp
from jax import lax

BASIS = 20
QUANTITIES = 27
FACE_BASIS = 10
ORDER = 4
ELEM_DEV = 512
LINK_STRIKE = 256
LINK_OTHER = 128
ELEMENTS = 131072
N_STRIKE = 16
N_DIP = 4
N_DEPTH = 4


def mesh_tables(key):
    devices = N_STRIKE * N_DIP * N_DEPTH
    elem_count = ELEM_DEV
    face_count = 4 * ELEM_DEV
    device_ids = jnp.arange(devices, dtype=jnp.int32)
    strides = [N_DIP * N_DEPTH, N_DEPTH, 1]
    extents = [N_STRIKE, N_DIP, N_DEPTH]
    limits = [LINK_STRIKE, LINK_OTHER, LINK_OTHER]
    count_cols = []
    for axis_index in range(3):
        position = device_ids // strides[axis_index] % extents[axis_index]
        drawn = 2 * jax.random.randint(jax.random.fold_in(key, 11 + axis_index), (devices,), limits[axis_index] // 4, limits[axis_index] // 2 + 1)
        drawn = drawn.astype(jnp.int32).at[0].set(limits[axis_index])
        plus_count = jnp.where(position < extents[axis_index] - 1, drawn, 0)
        lower_dev = jnp.clip(device_ids - strides[axis_index], 0, devices - 1)
        minus_count = jnp.where(position > 0, plus_count[lower_dev], 0)
        count_cols.append(plus_count)
        count_cols.append(minus_count)
    counts = jnp.stack(count_cols, axis=1).astype(jnp.int32)
    offsets = jnp.concatenate([jnp.zeros((devices, 1), jnp.int32), jnp.cumsum(counts, axis=1).astype(jnp.int32)], axis=1)
    sub_keys = jax.random.split(jax.random.fold_in(key, 21), devices)
    face_orders = jax.vmap(lambda sub_key: jax.random.permutation(sub_key, face_count))(sub_keys).astype(jnp.int32)
    positions = jnp.arange(face_count, dtype=jnp.int32)[None, :]
    direction = jnp.sum((positions[:, :, None] >= offsets[:, None, 1:]).astype(jnp.int32), axis=2)
    link_index = positions - jnp.take_along_axis(offsets, direction, axis=1)
    step_table = jnp.array([strides[0], -strides[0], strides[1], -strides[1], 1, -1, 0], jnp.int32)
    partner_table = jnp.array([1, 0, 3, 2, 5, 4, 6], jnp.int32)
    base_table = jnp.array([LINK_STRIKE, 0, 2 * LINK_STRIKE + LINK_OTHER, 2 * LINK_STRIKE, 2 * LINK_STRIKE + 3 * LINK_OTHER, 2 * LINK_STRIKE + 2 * LINK_OTHER, 0], jnp.int32)
    partner_dev = jnp.clip(device_ids[:, None] + step_table[direction], 0, devices - 1)
    partner_dir = partner_table[direction]
    inner_start = offsets[:, 6:7]
    remote_pos = offsets[partner_dev, partner_dir] + link_index
    inner_pos = inner_start + jnp.bitwise_xor(positions - inner_start, 1)
    is_remote = direction < 6
    partner_pos = jnp.clip(jnp.where(is_remote, remote_pos, inner_pos), 0, face_count - 1)
    partner_slot = face_orders[partner_dev, partner_pos]
    neighbour_code = jnp.where(is_remote, elem_count + base_table[direction] + link_index, partner_slot % elem_count)
    partner_face = partner_slot // elem_count
    inverse = jnp.argsort(face_orders, axis=1).astype(jnp.int32)

    def to_global(by_position):
        by_slot = jnp.take_along_axis(by_position, inverse, axis=1)
        return jnp.transpose(by_slot.reshape(devices, 4, elem_count), (1, 0, 2)).reshape(4, devices * elem_count).astype(jnp.int32)

    def exports(plus_dir, width):
        slot_ids = jnp.arange(width, dtype=jnp.int32)[None, :]
        export_rows = []
        for chosen in (plus_dir + 1, plus_dir):
            where_pos = jnp.clip(offsets[:, chosen:chosen + 1] + slot_ids, 0, face_count - 1)
            picked = jnp.take_along_axis(face_orders, where_pos, axis=1)
            export_rows.append(jnp.where(slot_ids < counts[:, chosen:chosen + 1], picked, 0))
        return jnp.stack(export_rows).reshape(2, devices * width).astype(jnp.int32)
    return (to_global(neighbour_code), to_global(partner_face), exports(0, LINK_STRIKE), exports(2, LINK_OTHER), exports(4, LINK_OTHER))


def draw_nb_index(key, part):
    tables = mesh_tables(key)
    return tables[0]


def draw_nb_face(key, part):
    tables = mesh_tables(key)
    return tables[1]


def draw_export_strike(key, part):
    tables = mesh_tables(key)
    return tables[2]


def draw_export_dip(key, part):
    tables = mesh_tables(key)
    return tables[3]


def draw_export_depth(key, part):
    tables = mesh_tables(key)
    return tables[4]


def plant(values, key, least, largest):
    shape = values.shape
    index_at = [jax.random.randint(jax.random.fold_in(key, axis), (), 0, shape[axis]) for axis in range(len(shape))]
    values = values.at[tuple(index_at)].set(least)
    longest = shape.index(max(shape))
    index_at[longest] = (index_at[longest] + 1) % shape[longest]
    return values.at[tuple(index_at)].set(largest)


def level_of(own_key, dims, cuts, least, high):
    loudness, own = 1.0, jax.random.fold_in(own_key, 6)
    for axis_at, shards_of in cuts:
        draws = jnp.exp(jax.random.uniform(jax.random.fold_in(own, axis_at), (shards_of,), jnp.float32, least / len(cuts), high / len(cuts)))
        loudness = loudness * jnp.repeat(draws, dims[axis_at] // shards_of).reshape([-1 if axis == axis_at else 1 for axis in range(len(dims))])
    return loudness


def normal_values(key, dims, scale, reach, cuts=(), kind=jnp.bfloat16):
    result = scale * jax.random.normal(key, dims, jnp.float32)
    if cuts:
        result = result * level_of(key, dims, cuts, -0.22, 0.18)
    return jnp.clip(result, -reach, reach).astype(kind)


def setup_inputs(seed: int = 0) -> dict:
    streams_of = jax.random.split(jax.random.key(seed), 18)
    return {
        "state": normal_values(streams_of[0], (BASIS, QUANTITIES, ELEMENTS), 1.0, 6.0, ((2, 256),), jnp.float32),
        "geometry": normal_values(streams_of[1], (3, 3, ELEMENTS), 1.0, 3.0, ((2, 256),), jnp.float32),
        "normals": normal_values(streams_of[2], (4, 3, ELEMENTS), 0.5, 3.0, ((2, 256),), jnp.float32),
        "wave_speed": jnp.clip(jnp.exp(math.log(2.0) - 1.3862944 * jax.random.uniform(streams_of[3], (ELEMENTS,), jnp.float32) ** level_of(streams_of[3], (ELEMENTS,), ((0, 256),), -0.2, 0.2)), 0.5, 2.0),
        "cluster": plant((jax.random.randint(streams_of[4], (ELEMENTS,), 0, 3) < 1).astype(jnp.int32), jax.random.fold_in(streams_of[4], 1), 0, 1),
        "nb_index": draw_nb_index(jax.random.fold_in(streams_of[17], 71), 0),
        "nb_face": draw_nb_face(jax.random.fold_in(streams_of[17], 71), 0),
        "orientation": plant(jax.random.randint(streams_of[7], (4, ELEMENTS), 0, 3), jax.random.fold_in(streams_of[7], 1), 0, 2).astype(jnp.int32),
        "export_strike": draw_export_strike(jax.random.fold_in(streams_of[17], 71), 0),
        "export_dip": draw_export_dip(jax.random.fold_in(streams_of[17], 71), 0),
        "export_depth": draw_export_depth(jax.random.fold_in(streams_of[17], 71), 0),
        "stiffness": normal_values(streams_of[11], (3, BASIS, BASIS), BASIS ** -0.5, 1.25, (), jnp.float32),
        "stiff_volume": normal_values(streams_of[12], (3, BASIS, BASIS), BASIS ** -0.5, 1.25, (), jnp.float32),
        "jacobians": normal_values(streams_of[13], (3, QUANTITIES, QUANTITIES), (3 * QUANTITIES) ** -0.5, 0.625, (), jnp.float32),
        "face_proj": normal_values(streams_of[14], (4, FACE_BASIS, BASIS), BASIS ** -0.5, 1.25, (), jnp.float32),
        "face_lift": normal_values(streams_of[15], (4, BASIS, FACE_BASIS), (4 * FACE_BASIS) ** -0.5, 1.0, (), jnp.float32),
        "rotations": normal_values(streams_of[16], (3, FACE_BASIS, FACE_BASIS), FACE_BASIS ** -0.5, 2.0, (), jnp.float32),
    }


time_step = 0.5
highest = lax.Precision.HIGHEST


def coefficients(cluster):
    is_fine = cluster == 0
    coef_rows = []
    for degree in range(ORDER):
        weight_base = time_step ** (degree + 1) / math.factorial(degree + 1)
        coarse_weight = weight_base * (2.0 ** (degree + 1) - 1.0)
        coef_rows.append(jnp.where(is_fine, jnp.float32(weight_base), jnp.float32(coarse_weight)))
    return jnp.stack(coef_rows)


def transport(field_in, matrices, geometry, jacobians):
    stiff_moved = jnp.einsum("dab,bqe->daqe", matrices, field_in, precision=highest)
    mixture = jnp.stack([geometry[0, j] * stiff_moved[0] + geometry[1, j] * stiff_moved[1] + geometry[2, j] * stiff_moved[2] for j in range(3)])
    return jnp.einsum("jaqe,jqp->ape", mixture, jacobians, precision=highest)


def predict(state, geometry, time_weights, stiffness, jacobians):
    derivative = state
    integral = time_weights[0] * state
    for degree in range(1, ORDER):
        derivative = -transport(derivative, stiffness, geometry, jacobians)
        integral = integral + time_weights[degree] * derivative
    return integral


def face_traces(integral, face_proj):
    elem_count = integral.shape[2]
    traces = jnp.einsum("fib,bqe->iqfe", face_proj, integral, precision=highest)
    return traces.reshape(face_proj.shape[1] * integral.shape[1], 4 * elem_count)


def finish(state, integral, geometry, normals, wave_speed, cluster, trace_pool, columns, orientation, stiff_volume, jacobians, face_lift, rotations):
    elem_count = state.shape[2]
    face_count = face_lift.shape[2]
    quantity_count = state.shape[1]
    own_traces = trace_pool[:, :4 * elem_count].reshape(face_count, quantity_count, 4 * elem_count)
    fetched = jnp.take(trace_pool, columns.reshape(-1), axis=1).reshape(face_count, quantity_count, 4 * elem_count)
    turn_codes = orientation.reshape(-1)
    neighbour = jnp.zeros_like(fetched)
    for turning in range(3):
        rotated = jnp.einsum("ij,jqx->iqx", rotations[turning], fetched, precision=highest)
        neighbour = jnp.where(turn_codes == turning, rotated, neighbour)
    summed = own_traces + neighbour
    face_jump = own_traces - neighbour
    face_normals = jnp.transpose(normals, (1, 0, 2)).reshape(3, 4 * elem_count)
    face_flux = 0.5 * jnp.tile(wave_speed, 4) * face_jump
    for direction in range(3):
        face_flux = face_flux + 0.5 * jnp.einsum("iqx,qp->ipx", face_normals[direction] * summed, jacobians[direction], precision=highest)
    lifted = jnp.einsum("fbi,ipfe->bpe", face_lift, face_flux.reshape(face_count, quantity_count, 4, elem_count), precision=highest)
    volume = transport(integral, stiff_volume, geometry, jacobians)
    update = jnp.where(cluster == 0, volume - lifted, 0.0)
    return state + update


def reference(state, geometry, normals, wave_speed, cluster, nb_index, nb_face, orientation, export_strike, export_dip, export_depth, stiffness, stiff_volume, jacobians, face_proj, face_lift, rotations):
    devices = N_STRIKE * N_DIP * N_DEPTH
    elem_count = ELEM_DEV

    def by_device(array, width):
        shaped = array.reshape(array.shape[:-1] + (devices, width))
        return jnp.moveaxis(shaped, -2, 0)

    states = by_device(state, elem_count)
    geometries = by_device(geometry, elem_count)
    normal_sets = by_device(normals, elem_count)
    speeds = by_device(wave_speed, elem_count)
    clusters = by_device(cluster, elem_count)
    indices = by_device(nb_index, elem_count)
    faces = by_device(nb_face, elem_count)
    turns = by_device(orientation, elem_count)
    strike_lists = by_device(export_strike, LINK_STRIKE)
    dip_lists = by_device(export_dip, LINK_OTHER)
    depth_lists = by_device(export_depth, LINK_OTHER)

    def first_pass(inputs):
        state_dev, geometry_dev, cluster_dev, strike_dev, dip_dev, depth_dev = inputs
        integral = predict(state_dev, geometry_dev, coefficients(cluster_dev), stiffness, jacobians)
        traces = face_traces(integral, face_proj)

        def select_slots(slot_lists):
            return jnp.moveaxis(jnp.take(traces, slot_lists, axis=1), 1, 0)

        return integral, select_slots(strike_dev), select_slots(dip_dev), select_slots(depth_dev)

    integrals, sent_strike, sent_dip, sent_depth = lax.map(first_pass, (states, geometries, clusters, strike_lists, dip_lists, depth_lists))

    def second_pass(inputs):
        device_id, state_dev, geometry_dev, normal_dev, speed_dev, cluster_dev, index_dev, face_dev, turn_dev, integral = inputs
        strike_pos = device_id // (N_DIP * N_DEPTH)
        dip_pos = (device_id // N_DEPTH) % N_DIP
        depth_pos = device_id % N_DEPTH

        def neighbour_rows(sent, offset, present, row_index):
            source = jnp.clip(device_id + offset, 0, devices - 1)
            return jnp.where(present, sent[source, row_index], 0.0)

        received = jnp.concatenate([
            neighbour_rows(sent_strike, -N_DIP * N_DEPTH, strike_pos > 0, 1),
            neighbour_rows(sent_strike, N_DIP * N_DEPTH, strike_pos < N_STRIKE - 1, 0),
            neighbour_rows(sent_dip, -N_DEPTH, dip_pos > 0, 1),
            neighbour_rows(sent_dip, N_DEPTH, dip_pos < N_DIP - 1, 0),
            neighbour_rows(sent_depth, -1, depth_pos > 0, 1),
            neighbour_rows(sent_depth, 1, depth_pos < N_DEPTH - 1, 0)], axis=1)
        trace_pool = jnp.concatenate([face_traces(integral, face_proj), received], axis=1)
        columns = jnp.where(index_dev < elem_count, face_dev * elem_count + index_dev, 3 * elem_count + index_dev)
        return finish(state_dev, integral, geometry_dev, normal_dev, speed_dev, cluster_dev, trace_pool, columns, turn_dev, stiff_volume, jacobians, face_lift, rotations)

    outputs = lax.map(second_pass, (jnp.arange(devices, dtype=jnp.int32), states, geometries, normal_sets, speeds, clusters, indices, faces, turns, integrals))
    return jnp.moveaxis(outputs, 0, -2).reshape(state.shape)
```

```python
import functools
import math

import jax
import jax.numpy as jnp
from jax import lax
from jax.experimental import pallas as pl
from jax.experimental.pallas import tpu as pltpu
from jax.sharding import PartitionSpec as P

MESH = pl.DeviceIdType.MESH
BASIS, QUANT, FACE = 20, 27, 10
ELEM = 512
TIME_STEP = 0.5
ORDER = 4
WIDE = 256
ROWS = 3
TRACE = 272
f32, bf16, i32 = jnp.float32, jnp.bfloat16, jnp.int32

LINKS = (
    ("strike", 0, 256),
    ("strike", 256, 256),
    ("dip", 512, 128),
    ("dip", 640, 128),
    ("depth", 768, 128),
    ("depth", 896, 128),
)


def dot(a, b):
    return jnp.dot(a, b, preferred_element_type=f32)


def split(x):
    high = x.astype(bf16)
    return high, (x - high.astype(f32)).astype(bf16)


def rep8(m):
    n, k = m.shape
    return jnp.broadcast_to(m[:, None, :], (n, 8, k)).reshape(n * 8, k)


def iota(shape, dim):
    return lax.broadcasted_iota(i32, shape, dim)


def spread(m, parts, count, first_part, last_part):
    n, k = m.shape
    width = parts * count * 8
    col = iota((k, width), 1)
    row = iota((k, width), 0)
    put = jnp.zeros((k, width), jnp.bool_)
    for part in range(first_part, last_part + 1):
        put = put | ((col - part * count * 8) >> 3 == row)
    wide = dot(rep8(m.astype(f32)).astype(bf16), jnp.where(put, 1.0, 0.0).astype(bf16))
    same = (iota((n * 8, width), 0) & 7) == (iota((n * 8, width), 1) & 7)
    return jnp.where(same, wide, 0.0)


def stacked(m, count):
    high, low = split(m)
    return (spread(high, 3, count, 0, 1) + spread(low, 3, count, 2, 2)).astype(bf16)


def jacobian_weights(jac_ref, tmp_ref, out_ref):
    tmp_ref[...] = jnp.zeros((128, 128), f32)
    for j in range(3):
        high, low = split(jac_ref[j])
        at = slice(32 * j, 32 * j + QUANT)
        tmp_ref[0:QUANT, at] = high.astype(f32)
        tmp_ref[32 : 32 + QUANT, at] = high.astype(f32)
        tmp_ref[64 : 64 + QUANT, at] = low.astype(f32)
    out_ref[...] = tmp_ref[...].T[:96, :96].astype(bf16)


def stiff_weights(mat_ref, sign, high_ref, low_ref):
    high_sum = jnp.zeros((160, 480), f32)
    low_sum = jnp.zeros((160, 480), f32)
    for d in range(3):
        high, low = split(sign * mat_ref[d])
        high_sum = high_sum + spread(high, 3, BASIS, d, d)
        low_sum = low_sum + spread(low, 3, BASIS, d, d)
    high_ref[...] = high_sum.astype(bf16)
    low_ref[...] = low_sum.astype(bf16)


def packed_project(m):
    high, low = split(m)
    row = iota((32, FACE), 0)
    third = (row * 171) >> 9
    pick = jnp.where(third == iota((32, FACE), 1), 1.0, 0.0).astype(bf16)
    total = jnp.zeros((32, 480), f32)
    for part_from, part_to, piece in ((0, 1, high), (2, 2, low)):
        rows = dot(pick, piece).astype(bf16)
        col = iota((BASIS, 480), 1)
        put = jnp.zeros((BASIS, 480), jnp.bool_)
        for part in range(part_from, part_to + 1):
            put = put | ((col - part * 160) >> 3 == iota((BASIS, 480), 0))
        total = total + dot(rows, jnp.where(put, 1.0, 0.0).astype(bf16))
    out_row = iota((32, 480), 0)
    same = (out_row - 3 * ((out_row * 171) >> 9)) == (iota((32, 480), 1) & 7)
    return jnp.where(same & (out_row < 30), total, 0.0).astype(bf16)


def packed_rotate(m):
    high, low = split(m)
    total = jnp.zeros((80, 96), f32)
    col = iota((FACE, 96), 1)
    for part_from, part_to, piece in ((0, 1, high), (2, 2, low)):
        put = jnp.zeros((FACE, 96), jnp.bool_)
        for part in range(part_from, part_to + 1):
            inner = col - part * 32
            put = put | ((inner >= 0) & (inner < 30) & ((inner * 171) >> 9 == iota((FACE, 96), 0)))
        total = total + dot(rep8(piece.astype(f32)).astype(bf16), jnp.where(put, 1.0, 0.0).astype(bf16))
    inner = iota((80, 96), 1) & 31
    same = (inner - 3 * ((inner * 171) >> 9)) == (iota((80, 96), 0) & 7)
    return jnp.where(same, total, 0.0).astype(bf16)


def mixed(field, geo, weights):
    high, low = split(field)
    moved = dot(weights, jnp.concatenate([high, low, high], axis=0))
    n = field.shape[1]
    parts = [moved[32 * j : 32 * j + 32].reshape(4, 8, n) for j in range(3)]
    return [
        (geo[d][0] * parts[0] + geo[d][1] * parts[1] + geo[d][2] * parts[2]).reshape(32, n)
        for d in range(3)
    ]


def transport(load, geo, jac_ref, high_ref, low_ref, mix_ref):
    for b in range(BASIS):
        for d, rows in enumerate(mixed(load(b), geo, jac_ref[...])):
            for s in range(4):
                at = (d * BASIS + b) * 8
                mix_ref[s, at : at + 8, :] = rows[8 * s : 8 * s + 8]
    slabs = []
    for s in range(4):
        high, low = split(mix_ref[s])
        weights_high = high_ref[...]
        slabs.append(dot(weights_high, high) + dot(weights_high, low) + dot(low_ref[...], high))
    return slabs


def kernel(
    remote,
    state_ref,
    geo_ref,
    nrm_ref,
    speed_ref,
    cluster_ref,
    nbi_ref,
    nbf_ref,
    orient_ref,
    exs_ref,
    exd_ref,
    exz_ref,
    stiff_ref,
    vol_ref,
    jac_ref,
    proj_ref,
    lift_ref,
    rot_ref,
    out_ref,
    field,
    integral,
    mix,
    own,
    total,
    mine,
    pool,
    ship,
    near,
    cols_v,
    cols_s,
    tmp,
    w_jac,
    w_stiff_h,
    w_stiff_l,
    w_vol_h,
    w_vol_l,
    w_proj,
    w_proj3,
    w_rot,
    w_rot3,
    w_lift,
    cols_sem,
    send_sem,
    recv_sem,
):
    links = []
    for at, (axis, first, rows) in enumerate(LINKS):
        step = -1 if at % 2 == 0 else 1
        if remote:
            pos, count = lax.axis_index(axis), lax.axis_size(axis)
            there = pos > 0 if step < 0 else pos < count - 1
            target = jnp.clip(pos + step, 0, count - 1)
        else:
            there, target = True, None
        land = first + rows if step < 0 else first - rows
        links.append((axis, step, there, target, first, land, rows))

    if remote:
        barrier = pltpu.get_barrier_semaphore()
        greeted = 0
        for axis, step, there, target, *_ in links:

            @pl.when(there)
            def _(axis=axis, target=target):
                pl.semaphore_signal(barrier, inc=1, device_id={axis: target}, device_id_type=MESH)

            greeted = greeted + there.astype(i32)

    index = nbi_ref[...]
    cols_v[...] = ROWS * jnp.where(index < ELEM, nbf_ref[...] * ELEM + index, 3 * ELEM + index)
    cols_copy = pltpu.make_async_copy(cols_v, cols_s, cols_sem)
    cols_copy.start()

    jacobian_weights(jac_ref, tmp, w_jac)
    stiff_weights(stiff_ref, -1.0, w_stiff_h, w_stiff_l)
    for f in range(4):
        w_proj[80 * f : 80 * f + 80] = stacked(proj_ref[f], BASIS)
        w_proj3[32 * f : 32 * f + 32] = packed_project(proj_ref[f])

    zeros5 = jnp.zeros((5, WIDE), f32)

    def columns(h):
        return pl.ds(pl.multiple_of(h * WIDE, WIDE), WIDE)

    def geometry(h):
        return [
            [jnp.broadcast_to(geo_ref[d, j : j + 1, columns(h)], (8, WIDE))[None] for j in range(3)]
            for d in range(3)
        ]

    def time_weights(h):
        fine = cluster_ref[:, columns(h)] == 0
        rows = []
        for degree in range(ORDER):
            base = TIME_STEP ** (degree + 1) / math.factorial(degree + 1)
            coarse = base * (2.0 ** (degree + 1) - 1.0)
            rows.append(jnp.broadcast_to(jnp.where(fine, f32(base), f32(coarse)), (8, WIDE)))
        return rows

    def slab(ref, s, h):
        return ref[:, 8 * s : 8 * s + 8, columns(h)].reshape(BASIS * 8, WIDE)

    def predict(h, carry):
        cs = columns(h)
        geo, times = geometry(h), time_weights(h)
        for b in range(BASIS):
            value = jnp.concatenate([state_ref[b, :, cs], zeros5], axis=0)
            field[b, :, cs] = value
            integral[b, :, cs] = (times[0][None] * value.reshape(4, 8, WIDE)).reshape(32, WIDE)
        for degree in range(1, ORDER):
            slabs = transport(lambda b: field[b, :, cs], geo, w_jac, w_stiff_h, w_stiff_l, mix)
            for s in range(4):
                value = slabs[s].reshape(BASIS, 8, WIDE)
                if degree < ORDER - 1:
                    field[:, 8 * s : 8 * s + 8, cs] = value
                integral[:, 8 * s : 8 * s + 8, cs] += times[degree][None] * value
        for s in range(4):
            high, low = split(slab(integral, s, h))
            operand = jnp.concatenate([high, low, high], axis=0)
            traces = dot(w_proj[...], operand)
            for f in range(4):
                part = traces[80 * f : 80 * f + 80]
                own[f, :, 8 * s : 8 * s + 8, cs] = part.reshape(FACE, 8, WIDE)
            if s == 3:
                packed = dot(w_proj3[...], operand)
        for f in range(4):
            pieces = [
                own[f, :, 8 * s : 8 * s + 8, cs].reshape(80, WIDE) for s in range(3)
            ] + [packed[32 * f : 32 * f + 32]]
            whole = jnp.concatenate(pieces, axis=0)
            for t in range(WIDE // 128):
                lanes = slice(128 * t, 128 * t + 128)
                base = ROWS * (f * ELEM + 128 * t) + ROWS * WIDE * h
                for c in range(ROWS):
                    chunk = whole[128 * c : min(128 * c + 128, TRACE), lanes]
                    if c == ROWS - 1:
                        chunk = jnp.concatenate([chunk, jnp.zeros((128 - chunk.shape[0], 128), f32)], axis=0)
                    turned = chunk.T
                    mine[pl.ds(base + c, 128, stride=ROWS), :] = turned
                    pool[pl.ds(base + c, 128, stride=ROWS), :] = turned
        return carry

    lax.fori_loop(0, ELEM // WIDE, predict, 0)

    if remote:
        pl.semaphore_wait(barrier, greeted)

    copies = []
    for at, (axis, step, there, target, first, land, rows) in enumerate(links):
        ref = (exs_ref, exd_ref, exz_ref)[at // 2]
        side = at % 2

        def export(t, carry, ref=ref, side=side, first=first):
            for u in range(16):
                slot = ref[side, t * 16 + u]
                ship[pl.ds(ROWS * (first + t * 16 + u), ROWS), :] = mine[pl.ds(ROWS * slot, ROWS), :]
            return carry

        lax.fori_loop(0, rows // 16, export, 0)
        source = ship.at[pl.ds(ROWS * first, ROWS * rows), :]
        goal = pool.at[pl.ds(ROWS * (4 * ELEM + land), ROWS * rows), :]
        if remote:
            other = at ^ 1
            copy = pltpu.make_async_remote_copy(
                src_ref=source,
                dst_ref=goal,
                send_sem=send_sem.at[at],
                recv_sem=recv_sem.at[other],
                device_id={axis: target},
                device_id_type=MESH,
            )
            pl.when(there)(copy.start)
        else:
            copy = pltpu.make_async_copy(source, goal, send_sem.at[at])
            copy.start()
        copies.append(copy)

    stiff_weights(vol_ref, 1.0, w_vol_h, w_vol_l)
    for o in range(3):
        w_rot[80 * o : 80 * o + 80] = stacked(rot_ref[o], FACE)
        w_rot3[80 * o : 80 * o + 80] = packed_rotate(rot_ref[o])
    for f in range(4):
        w_lift[f] = stacked(-lift_ref[f], FACE)

    def volume(h, carry):
        cs = columns(h)
        slabs = transport(lambda b: integral[b, :, cs], geometry(h), w_jac, w_vol_h, w_vol_l, mix)
        for s in range(4):
            total[s, :, cs] = slabs[s]
        return carry

    lax.fori_loop(0, ELEM // WIDE, volume, 0)
    cols_copy.wait()

    for at, (axis, step, there, target, first, land, rows) in enumerate(links):
        copy = copies[at]
        if remote:
            arrived = pltpu.make_async_remote_copy(
                src_ref=ship.at[pl.ds(ROWS * first, ROWS * rows), :],
                dst_ref=pool.at[pl.ds(ROWS * (4 * ELEM + first), ROWS * rows), :],
                send_sem=send_sem.at[at],
                recv_sem=recv_sem.at[at],
                device_id={axis: target},
                device_id_type=MESH,
            )

            @pl.when(there)
            def _(copy=copy, arrived=arrived):
                copy.wait_send()
                arrived.wait_recv()
        else:
            copy.wait()

    def faces(step, carry):
        f, h = step // 2, step % 2
        cs = columns(h)

        def fetch(t, inner):
            for u in range(16):
                at = cols_s[f, h * WIDE + t * 16 + u]
                near[pl.ds(t * 16 + u, ROWS, stride=WIDE), :] = pool[pl.ds(at, ROWS), :]
            return inner

        lax.fori_loop(0, WIDE // 16, fetch, 0)
        halves = []
        for t in range(WIDE // 128):
            turned = [near[WIDE * c + 128 * t : WIDE * c + 128 * t + 128, :].T for c in range(ROWS)]
            halves.append(jnp.concatenate([turned[0], turned[1], turned[2][: TRACE - 256]], axis=0))
        high, low = split(jnp.concatenate(halves, axis=1))
        turn = jnp.broadcast_to(orient_ref[pl.ds(f, 1), cs], (8, WIDE))[None]
        nb = []
        for s in range(4):
            rows = slice(80 * s, min(80 * s + 80, TRACE))
            operand = jnp.concatenate([high[rows], low[rows], high[rows]], axis=0)
            turned = dot(w_rot[...] if s < 3 else w_rot3[...], operand).reshape(3, FACE, 8, WIDE)
            nb.append(jnp.where(turn == 0, turned[0], jnp.where(turn == 1, turned[1], turned[2])))
        normal = [
            0.5 * jnp.broadcast_to(nrm_ref[f, j : j + 1, cs], (8, WIDE))[None] for j in range(3)
        ]
        speed = 0.5 * jnp.broadcast_to(speed_ref[:, cs], (8, WIDE))[None]
        flux = []
        for i in range(FACE):
            there = jnp.stack([nb[s][i] for s in range(4)])
            here = own[f, i, :, cs].reshape(4, 8, WIDE)
            high, low = split((here + there).reshape(32, WIDE))
            moved = dot(w_jac[...], jnp.concatenate([high, low, high], axis=0))
            value = speed * (here - there)
            for j in range(3):
                value = value + normal[j] * moved[32 * j : 32 * j + 32].reshape(4, 8, WIDE)
            flux.append(value)
        for s in range(4):
            high, low = split(jnp.concatenate([flux[i][s] for i in range(FACE)], axis=0))
            operand = jnp.concatenate([high, low, high], axis=0)
            total[s, :, cs] += dot(w_lift[f], operand)
        return carry

    lax.fori_loop(0, 8, faces, 0)

    for h in range(ELEM // WIDE):
        cs = slice(h * WIDE, h * WIDE + WIDE)
        fine = jnp.broadcast_to(cluster_ref[:, cs], (8, WIDE)) == 0
        for b in range(BASIS):
            for s in range(4):
                n = min(8, QUANT - 8 * s)
                update = jnp.where(fine, total[s, 8 * b : 8 * b + 8, cs], 0.0)[:n]
                out_ref[b, 8 * s : 8 * s + n, cs] = state_ref[b, 8 * s : 8 * s + n, cs] + update


def update_call(remote, *args):
    vmem = pl.BlockSpec(memory_space=pltpu.VMEM)
    smem = pl.BlockSpec(memory_space=pltpu.SMEM)
    return pl.pallas_call(
        functools.partial(kernel, remote),
        out_shape=jax.ShapeDtypeStruct((BASIS, QUANT, ELEM), f32),
        in_specs=[vmem] * 8 + [smem] * 3 + [vmem] * 6,
        out_specs=vmem,
        scratch_shapes=[
            pltpu.VMEM((BASIS, 32, ELEM), f32),
            pltpu.VMEM((BASIS, 32, ELEM), f32),
            pltpu.VMEM((4, 480, WIDE), f32),
            pltpu.VMEM((4, FACE, 32, ELEM), f32),
            pltpu.VMEM((4, 160, ELEM), f32),
            pltpu.VMEM((ROWS * 4 * ELEM, 128), f32),
            pltpu.VMEM((ROWS * 6 * ELEM, 128), f32),
            pltpu.VMEM((ROWS * 2 * ELEM, 128), f32),
            pltpu.VMEM((ROWS * WIDE, 128), f32),
            pltpu.VMEM((4, ELEM), i32),
            pltpu.SMEM((4, ELEM), i32),
            pltpu.VMEM((128, 128), f32),
            pltpu.VMEM((96, 96), bf16),
            pltpu.VMEM((160, 480), bf16),
            pltpu.VMEM((160, 480), bf16),
            pltpu.VMEM((160, 480), bf16),
            pltpu.VMEM((160, 480), bf16),
            pltpu.VMEM((320, 480), bf16),
            pltpu.VMEM((128, 480), bf16),
            pltpu.VMEM((240, 240), bf16),
            pltpu.VMEM((240, 96), bf16),
            pltpu.VMEM((4, 160, 240), bf16),
            pltpu.SemaphoreType.DMA,
            pltpu.SemaphoreType.DMA((6,)),
            pltpu.SemaphoreType.DMA((6,)),
        ],
        compiler_params=pltpu.CompilerParams(
            vmem_limit_bytes=56 * 2**20,
            **(dict(collective_id=0, has_side_effects=True) if remote else {}),
        ),
    )(*args)


def per_device(state, geometry, normals, wave_speed, cluster, *rest):
    return update_call(
        True, state, geometry, normals, wave_speed.reshape(1, ELEM), cluster.reshape(1, ELEM), *rest
    )


def solution(mesh):
    whole = ("strike", "dip", "depth")
    placed = (
        (P(None, None, whole),) * 3 + (P(whole),) * 2 + (P(None, whole),) * 6 + (P(),) * 6
    )
    return jax.shard_map(
        per_device,
        mesh=mesh,
        in_specs=placed,
        out_specs=P(None, None, whole),
        check_vma=False,
    )
```

```python
import functools
import math

import jax
import jax.numpy as jnp
from jax import lax
from jax.experimental import pallas as pl
from jax.experimental.pallas import tpu as pltpu
from jax.sharding import PartitionSpec as P

MESH = pl.DeviceIdType.MESH
BASIS, QUANT, FACE = 20, 27, 10
ELEM = 512
TIME_STEP = 0.5
ORDER = 4
WIDE = 256
ROWS = 3
TRACE = 272
f32, bf16, i32 = jnp.float32, jnp.bfloat16, jnp.int32

LINKS = (
    ("strike", 0, 256),
    ("strike", 256, 256),
    ("dip", 512, 128),
    ("dip", 640, 128),
    ("depth", 768, 128),
    ("depth", 896, 128),
)


def dot(a, b):
    return jnp.dot(a, b, preferred_element_type=f32)


def split(x):
    high = x.astype(bf16)
    return high, (x - high.astype(f32)).astype(bf16)


def rep8(m):
    n, k = m.shape
    return jnp.broadcast_to(m[:, None, :], (n, 8, k)).reshape(n * 8, k)


def iota(shape, dim):
    return lax.broadcasted_iota(i32, shape, dim)


def spread(m, parts, count, chosen):
    n, k = m.shape
    width = parts * count * 8
    col = iota((k, width), 1)
    row = iota((k, width), 0)
    put = jnp.zeros((k, width), jnp.bool_)
    for part in chosen:
        put = put | ((col - part * count * 8) >> 3 == row)
    wide = dot(rep8(m.astype(f32)).astype(bf16), jnp.where(put, 1.0, 0.0).astype(bf16))
    same = (iota((n * 8, width), 0) & 7) == (iota((n * 8, width), 1) & 7)
    return jnp.where(same, wide, 0.0)


def stacked(m, count):
    high, low = split(m)
    return (spread(high, 3, count, (0, 1)) + spread(low, 3, count, (2,))).astype(bf16)


def jacobian_weights(jac_ref, tmp_ref, out_ref):
    tmp_ref[...] = jnp.zeros((128, 128), f32)
    for j in range(3):
        high, low = split(jac_ref[j])
        at = slice(32 * j, 32 * j + QUANT)
        tmp_ref[0:QUANT, at] = high.astype(f32)
        tmp_ref[32 : 32 + QUANT, at] = high.astype(f32)
        tmp_ref[64 : 64 + QUANT, at] = low.astype(f32)
    out_ref[...] = tmp_ref[...].T[:96, :96].astype(bf16)


def stiff_weights(mat_ref, sign, high_ref, low_ref):
    high_sum = jnp.zeros((160, 960), f32)
    low_sum = jnp.zeros((160, 480), f32)
    for d in range(3):
        high, low = split(sign * mat_ref[d])
        high_sum = high_sum + spread(high, 6, BASIS, (d, d + 3))
        low_sum = low_sum + spread(low, 3, BASIS, (d,))
    high_ref[...] = high_sum.astype(bf16)
    low_ref[...] = low_sum.astype(bf16)


def packed_project(m):
    high, low = split(m)
    row = iota((32, FACE), 0)
    third = (row * 171) >> 9
    pick = jnp.where(third == iota((32, FACE), 1), 1.0, 0.0).astype(bf16)
    total = jnp.zeros((32, 480), f32)
    for part_from, part_to, piece in ((0, 1, high), (2, 2, low)):
        rows = dot(pick, piece).astype(bf16)
        col = iota((BASIS, 480), 1)
        put = jnp.zeros((BASIS, 480), jnp.bool_)
        for part in range(part_from, part_to + 1):
            put = put | ((col - part * 160) >> 3 == iota((BASIS, 480), 0))
        total = total + dot(rows, jnp.where(put, 1.0, 0.0).astype(bf16))
    out_row = iota((32, 480), 0)
    same = (out_row - 3 * ((out_row * 171) >> 9)) == (iota((32, 480), 1) & 7)
    return jnp.where(same & (out_row < 30), total, 0.0).astype(bf16)


def packed_rotate(m):
    high, low = split(m)
    total = jnp.zeros((80, 96), f32)
    col = iota((FACE, 96), 1)
    for part_from, part_to, piece in ((0, 1, high), (2, 2, low)):
        put = jnp.zeros((FACE, 96), jnp.bool_)
        for part in range(part_from, part_to + 1):
            inner = col - part * 32
            put = put | ((inner >= 0) & (inner < 30) & ((inner * 171) >> 9 == iota((FACE, 96), 0)))
        total = total + dot(rep8(piece.astype(f32)).astype(bf16), jnp.where(put, 1.0, 0.0).astype(bf16))
    inner = iota((80, 96), 1) & 31
    same = (inner - 3 * ((inner * 171) >> 9)) == (iota((80, 96), 0) & 7)
    return jnp.where(same, total, 0.0).astype(bf16)


def mixed(field, geo, weights):
    high, low = split(field)
    moved = dot(weights, jnp.concatenate([high, low, high], axis=0))
    n = field.shape[1]
    parts = [moved[32 * j : 32 * j + 32].reshape(4, 8, n) for j in range(3)]
    return [
        (geo[d][0] * parts[0] + geo[d][1] * parts[1] + geo[d][2] * parts[2]).reshape(32, n)
        for d in range(3)
    ]


def mix_steps(load, geo, jac_ref, mix_ref):
    def step(b):
        first, second = (mixed(load(b + i), geo, jac_ref[...]) for i in range(2))
        for d in range(3):
            for s in range(4):
                rows = slice(8 * s, 8 * s + 8)
                high, low = split(jnp.concatenate([first[d][rows], second[d][rows]], axis=0))
                at = (d * BASIS + b) * 8
                mix_ref[s, at : at + 16, :] = high
                mix_ref[s, 480 + at : 480 + at + 16, :] = low

    return [functools.partial(step, b) for b in range(0, BASIS, 2)]


def stiff_steps(mix_ref, weights_ref, low_ref, store):
    def step(s):
        store(s, dot(weights_ref[...], mix_ref[s]) + dot(low_ref[...], mix_ref[s, :480]))

    return [functools.partial(step, s) for s in range(4)]


def run(*phases):
    for phase in phases:
        for step in phase:
            step()


def kernel(
    remote,
    state_ref,
    geo_ref,
    nrm_ref,
    speed_ref,
    cluster_ref,
    nbi_ref,
    nbf_ref,
    orient_ref,
    exs_ref,
    exd_ref,
    exz_ref,
    stiff_ref,
    vol_ref,
    jac_ref,
    proj_ref,
    lift_ref,
    rot_ref,
    out_ref,
    field_a,
    field_b,
    integral_a,
    integral_b,
    mix_a,
    mix_b,
    times,
    own,
    total,
    mine,
    pool,
    ship,
    near,
    cols_v,
    cols_s,
    exp_v,
    exp_s,
    tmp,
    tmp2,
    w_jac,
    w_stiff_h,
    w_stiff_l,
    w_vol_h,
    w_vol_l,
    w_proj,
    w_proj3,
    w_rot,
    w_rot3,
    w_lift,
    cols_sem,
    send_sem,
    recv_sem,
):
    fields, integrals, mixes = (field_a, field_b), (integral_a, integral_b), (mix_a, mix_b)
    halves = range(ELEM // WIDE)

    links = []
    for at, (axis, first, rows) in enumerate(LINKS):
        step = -1 if at % 2 == 0 else 1
        if remote:
            pos, count = lax.axis_index(axis), lax.axis_size(axis)
            there = pos > 0 if step < 0 else pos < count - 1
            target = jnp.clip(pos + step, 0, count - 1)
        else:
            there, target = True, None
        land = first + rows if step < 0 else first - rows
        links.append((axis, there, target, first, land, rows))

    if remote:
        barrier = pltpu.get_barrier_semaphore()
        greeted = 0
        for axis, there, target, *_ in links:

            @pl.when(there)
            def _(axis=axis, target=target):
                pl.semaphore_signal(barrier, inc=1, device_id={axis: target}, device_id_type=MESH)

            greeted = greeted + there.astype(i32)

    index = nbi_ref[...]
    cols_v[...] = ROWS * jnp.where(index < ELEM, nbf_ref[...] * ELEM + index, 3 * ELEM + index)
    exp_v[:, 0:256] = ROWS * exs_ref[...]
    exp_v[:, 256:384] = ROWS * exd_ref[...]
    exp_v[:, 384:512] = ROWS * exz_ref[...]
    index_copies = [
        pltpu.make_async_copy(cols_v, cols_s, cols_sem.at[0]),
        pltpu.make_async_copy(exp_v, exp_s, cols_sem.at[1]),
    ]
    for copy in index_copies:
        copy.start()

    jacobian_weights(jac_ref, tmp, w_jac)
    stiff_weights(stiff_ref, -1.0, w_stiff_h, w_stiff_l)
    for f in range(4):
        w_proj[80 * f : 80 * f + 80] = stacked(proj_ref[:, f, :], BASIS)
        w_proj3[32 * f : 32 * f + 32] = packed_project(proj_ref[:, f, :])

    zeros5 = jnp.zeros((5, WIDE), f32)

    def columns(h):
        return slice(h * WIDE, h * WIDE + WIDE)

    def geometry(h):
        return [
            [jnp.broadcast_to(geo_ref[d, j : j + 1, columns(h)], (8, WIDE))[None] for j in range(3)]
            for d in range(3)
        ]

    fine = cluster_ref[...] == 0
    for degree in range(ORDER):
        base = TIME_STEP ** (degree + 1) / math.factorial(degree + 1)
        coarse = base * (2.0 ** (degree + 1) - 1.0)
        times[degree] = jnp.broadcast_to(jnp.where(fine, f32(base), f32(coarse)), (8, ELEM))

    for h in halves:
        for b in range(BASIS):
            value = jnp.concatenate([state_ref[b, :, columns(h)], zeros5], axis=0)
            fields[h][b] = value
            integrals[h][b] = (times[0, :, columns(h)][None] * value.reshape(4, 8, WIDE)).reshape(32, WIDE)

    def predict(degree, carry):
        phases = [mix_steps(lambda b, h=h: fields[h][b], geometry(h), w_jac, mixes[h]) for h in halves]
        for h in halves:

            def store(s, value, h=h):
                value = value.reshape(BASIS, 8, WIDE)
                rows = slice(8 * s, 8 * s + 8)
                fields[h][:, rows, :] = value
                integrals[h][:, rows, :] += times[degree, :, columns(h)][None] * value

            phases.append(stiff_steps(mixes[h], w_stiff_h, w_stiff_l, store))
        run(*phases)
        return carry

    lax.fori_loop(1, ORDER, predict, 0)

    for h in halves:
        for s in range(4):
            high, low = split(integrals[h][:, 8 * s : 8 * s + 8, :].reshape(BASIS * 8, WIDE))
            operand = jnp.concatenate([high, low, high], axis=0)
            traces = dot(w_proj[...], operand)
            for f in range(4):
                own[f, :, 8 * s : 8 * s + 8, columns(h)] = traces[80 * f : 80 * f + 80].reshape(FACE, 8, WIDE)
            if s == 3:
                packed = dot(w_proj3[...], operand)
        for f in range(4):
            pieces = [own[f, :, 8 * s : 8 * s + 8, columns(h)].reshape(80, WIDE) for s in range(3)]
            whole = jnp.concatenate(pieces + [packed[32 * f : 32 * f + 32]], axis=0)
            for t in range(WIDE // 128):
                base = ROWS * (f * ELEM + h * WIDE + 128 * t)
                for c in range(ROWS):
                    chunk = whole[128 * c : min(128 * c + 128, TRACE), 128 * t : 128 * t + 128]
                    if c == ROWS - 1:
                        chunk = jnp.concatenate([chunk, jnp.zeros((128 - chunk.shape[0], 128), f32)], axis=0)
                    turned = chunk.T
                    mine[pl.ds(base + c, 128, stride=ROWS), :] = turned
                    pool[pl.ds(base + c, 128, stride=ROWS), :] = turned

    for copy in index_copies:
        copy.wait()
    if remote:
        pl.semaphore_wait(barrier, greeted)

    copies = []
    for at, (axis, there, target, first, land, rows) in enumerate(links):
        side = at % 2
        lane = (0, 256, 384)[at // 2]

        def export(t, carry, side=side, first=first, lane=lane):
            for u in range(64):
                row = exp_s[side, lane + t * 64 + u]
                ship[pl.ds(ROWS * (first + t * 64 + u), ROWS), :] = mine[pl.ds(row, ROWS), :]
            return carry

        lax.fori_loop(0, rows // 64, export, 0)
        source = ship.at[pl.ds(ROWS * first, ROWS * rows), :]
        goal = pool.at[pl.ds(ROWS * (4 * ELEM + land), ROWS * rows), :]
        if remote:
            copy = pltpu.make_async_remote_copy(
                src_ref=source,
                dst_ref=goal,
                send_sem=send_sem.at[at],
                recv_sem=recv_sem.at[at ^ 1],
                device_id={axis: target},
                device_id_type=MESH,
            )
            pl.when(there)(copy.start)
        else:
            copy = pltpu.make_async_copy(source, goal, send_sem.at[at])
            copy.start()
        copies.append(copy)

    stiff_weights(vol_ref, 1.0, w_vol_h, w_vol_l)
    tmp2[...] = jnp.zeros((128, 128), f32)
    for f in range(4):
        tmp2[16 * f : 16 * f + FACE, 0:BASIS] = lift_ref[:, f, :]
    lifts = tmp2[...].T
    for o in range(3):
        w_rot[80 * o : 80 * o + 80] = stacked(rot_ref[:, o, :], FACE)
        w_rot3[80 * o : 80 * o + 80] = packed_rotate(rot_ref[:, o, :])
    for f in range(4):
        w_lift[f] = stacked(-lifts[0:BASIS, 16 * f : 16 * f + FACE], FACE)

    phases = [mix_steps(lambda b, h=h: integrals[h][b], geometry(h), w_jac, mixes[h]) for h in halves]
    for h in halves:

        def store(s, value, h=h):
            total[s, :, columns(h)] = value

        phases.append(stiff_steps(mixes[h], w_vol_h, w_vol_l, store))
    run(*phases)

    for at, (axis, there, target, first, land, rows) in enumerate(links):
        copy = copies[at]
        if remote:
            arrived = pltpu.make_async_remote_copy(
                src_ref=ship.at[pl.ds(ROWS * first, ROWS * rows), :],
                dst_ref=pool.at[pl.ds(ROWS * (4 * ELEM + first), ROWS * rows), :],
                send_sem=send_sem.at[at],
                recv_sem=recv_sem.at[at],
                device_id={axis: target},
                device_id_type=MESH,
            )

            @pl.when(there)
            def _(copy=copy, arrived=arrived):
                copy.wait_send()
                arrived.wait_recv()
        else:
            copy.wait()

    def fetch(f, first, count):
        for n in range(first, first + count):
            near[pl.ds(ROWS * n, ROWS), :] = pool[pl.ds(cols_s[f, n], ROWS), :]

    def turned(f, h):
        tiles = []
        for t in range(WIDE // 128):
            base = ROWS * (h * WIDE + 128 * t)
            parts = [near[pl.ds(base + c, 128, stride=ROWS), :].T for c in range(ROWS)]
            tiles.append(jnp.concatenate([parts[0], parts[1], parts[2][: TRACE - 256]], axis=0))
        high, low = split(jnp.concatenate(tiles, axis=1))
        turn = jnp.broadcast_to(orient_ref[pl.ds(f, 1), columns(h)], (8, WIDE))[None]
        slabs = []
        for s in range(4):
            rows = slice(80 * s, min(80 * s + 80, TRACE))
            operand = jnp.concatenate([high[rows], low[rows], high[rows]], axis=0)
            ways = dot(w_rot[...] if s < 3 else w_rot3[...], operand).reshape(3, FACE, 8, WIDE)
            slabs.append(jnp.where(turn == 0, ways[0], jnp.where(turn == 1, ways[1], ways[2])))
        return slabs

    def fluxes(f, h, slabs):
        normal = [
            0.5 * jnp.broadcast_to(nrm_ref[j, pl.ds(f, 1), columns(h)], (8, WIDE))[None] for j in range(3)
        ]
        speed = 0.5 * jnp.broadcast_to(speed_ref[:, columns(h)], (8, WIDE))[None]
        flux = []
        for i in range(FACE):
            there = jnp.stack([slabs[s][i] for s in range(4)])
            here = own[f, i, :, columns(h)].reshape(4, 8, WIDE)
            high, low = split((here + there).reshape(32, WIDE))
            moved = dot(w_jac[...], jnp.concatenate([high, low, high], axis=0))
            value = speed * (here - there)
            for j in range(3):
                value = value + normal[j] * moved[32 * j : 32 * j + 32].reshape(4, 8, WIDE)
            flux.append(value)
        return flux

    def lifted(f, h, flux):
        for s in range(4):
            high, low = split(jnp.concatenate([flux[i][s] for i in range(FACE)], axis=0))
            operand = jnp.concatenate([high, low, high], axis=0)
            total[s, :, columns(h)] += dot(w_lift[f], operand)

    fetch(0, 0, ELEM)

    def faces(f, carry):
        later = jnp.minimum(f + 1, 3)
        slabs = [turned(f, h) for h in halves]
        flux = []
        for h in halves:
            flux.append(fluxes(f, h, slabs[h]))
            fetch(later, h * (ELEM // 4), ELEM // 4)
        for h in halves:
            lifted(f, h, flux[h])
            fetch(later, ELEM // 2 + h * (ELEM // 4), ELEM // 4)
        return carry

    lax.fori_loop(0, 4, faces, 0)

    for h in halves:
        keep = jnp.broadcast_to(cluster_ref[:, columns(h)], (8, WIDE)) == 0
        for b in range(BASIS):
            for s in range(4):
                n = min(8, QUANT - 8 * s)
                update = jnp.where(keep, total[s, 8 * b : 8 * b + 8, columns(h)], 0.0)[:n]
                out_ref[b, 8 * s : 8 * s + n, columns(h)] = (
                    state_ref[b, 8 * s : 8 * s + n, columns(h)] + update
                )


def update_call(remote, *args):
    vmem = pl.BlockSpec(memory_space=pltpu.VMEM)
    return pl.pallas_call(
        functools.partial(kernel, remote),
        out_shape=pltpu.VMEM((BASIS, QUANT, ELEM), f32),
        in_specs=[vmem] * 17,
        out_specs=vmem,
        scratch_shapes=[
            pltpu.VMEM((BASIS, 32, WIDE), f32),
            pltpu.VMEM((BASIS, 32, WIDE), f32),
            pltpu.VMEM((BASIS, 32, WIDE), f32),
            pltpu.VMEM((BASIS, 32, WIDE), f32),
            pltpu.VMEM((4, 960, WIDE), bf16),
            pltpu.VMEM((4, 960, WIDE), bf16),
            pltpu.VMEM((ORDER, 8, ELEM), f32),
            pltpu.VMEM((4, FACE, 32, ELEM), f32),
            pltpu.VMEM((4, 160, ELEM), f32),
            pltpu.VMEM((ROWS * 4 * ELEM, 128), f32),
            pltpu.VMEM((ROWS * 6 * ELEM, 128), f32),
            pltpu.VMEM((ROWS * 2 * ELEM, 128), f32),
            pltpu.VMEM((ROWS * ELEM, 128), f32),
            pltpu.VMEM((4, ELEM), i32),
            pltpu.SMEM((4, ELEM), i32),
            pltpu.VMEM((2, ELEM), i32),
            pltpu.SMEM((2, ELEM), i32),
            pltpu.VMEM((128, 128), f32),
            pltpu.VMEM((128, 128), f32),
            pltpu.VMEM((96, 96), bf16),
            pltpu.VMEM((160, 960), bf16),
            pltpu.VMEM((160, 480), bf16),
            pltpu.VMEM((160, 960), bf16),
            pltpu.VMEM((160, 480), bf16),
            pltpu.VMEM((320, 480), bf16),
            pltpu.VMEM((128, 480), bf16),
            pltpu.VMEM((240, 240), bf16),
            pltpu.VMEM((240, 96), bf16),
            pltpu.VMEM((4, 160, 240), bf16),
            pltpu.SemaphoreType.DMA((2,)),
            pltpu.SemaphoreType.DMA((6,)),
            pltpu.SemaphoreType.DMA((6,)),
        ],
        compiler_params=pltpu.CompilerParams(
            vmem_limit_bytes=56 * 2**20,
            **(dict(collective_id=0, has_side_effects=True) if remote else {}),
        ),
    )(*args)


def arranged(args):
    state, geometry, normals, speed, cluster, *rest, proj, lift, rot = args
    return (
        state,
        geometry,
        jnp.transpose(normals, (1, 0, 2)),
        speed.reshape(1, ELEM),
        cluster.reshape(1, ELEM),
        *rest,
        jnp.transpose(proj, (1, 0, 2)),
        jnp.transpose(lift, (2, 0, 1)),
        jnp.transpose(rot, (1, 0, 2)),
    )


def per_device(*args):
    return update_call(True, *arranged(args))


def solution(mesh):
    whole = ("strike", "dip", "depth")
    placed = (
        (P(None, None, whole),) * 3 + (P(whole),) * 2 + (P(None, whole),) * 6 + (P(),) * 6
    )
    return jax.shard_map(
        per_device,
        mesh=mesh,
        in_specs=placed,
        out_specs=P(None, None, whole),
        check_vma=False,
    )
```

```python
import functools
import math

import jax
import jax.numpy as jnp
from jax import lax
from jax.experimental import pallas as pl
from jax.experimental.pallas import tpu as pltpu
from jax.sharding import PartitionSpec as P

MESH = pl.DeviceIdType.MESH
BASIS, QUANT, FACE = 20, 27, 10
ELEM = 512
TIME_STEP = 0.5
ORDER = 4
WIDE = 256
ROWS = 3
TRACE = 272
f32, bf16, i32 = jnp.float32, jnp.bfloat16, jnp.int32

LINKS = (
    ("strike", 0, 256),
    ("strike", 256, 256),
    ("dip", 512, 128),
    ("dip", 640, 128),
    ("depth", 768, 128),
    ("depth", 896, 128),
)


def dot(a, b):
    return jnp.dot(a, b, preferred_element_type=f32)


def split(x):
    high = x.astype(bf16)
    return high, (x - high.astype(f32)).astype(bf16)


def rep8(m):
    n, k = m.shape
    return jnp.broadcast_to(m[:, None, :], (n, 8, k)).reshape(n * 8, k)


def iota(shape, dim):
    return lax.broadcasted_iota(i32, shape, dim)


def ones_where(mask):
    return jnp.where(mask, 1.0, 0.0).astype(bf16)


def expander(count):
    shape = (96, 24 * count)
    row, entry = iota(shape, 0), iota(shape, 1) >> 3
    part = row >> 5
    inner = row & 31
    return ones_where((inner < count) & (entry == part * count + inner))


def diagonal(width):
    return (iota((8, width), 0) == (iota((8, width), 1) & 7))[None]


def kron8(rows, expand, diag):
    n, width = rows.shape[0], expand.shape[1]
    wide = dot(rep8(rows).astype(bf16), expand).reshape(n, 8, width)
    return jnp.where(diag, wide, 0.0).reshape(n * 8, width).astype(bf16)


def lay(tmp_ref, at, m):
    n, k = m.shape
    high, low = (piece.astype(f32) for piece in split(m))
    for part, piece in enumerate((high, high, low)):
        tmp_ref[at : at + n, 32 * part : 32 * part + k] = piece


def third(x):
    return (x * 171) >> 9


def jacobian_weights(jac_ref, tmp_ref, out_ref):
    for j in range(3):
        high, low = split(jac_ref[j])
        at = slice(32 * j, 32 * j + QUANT)
        tmp_ref[0:QUANT, at] = high.astype(f32)
        tmp_ref[32 : 32 + QUANT, at] = high.astype(f32)
        tmp_ref[64 : 64 + QUANT, at] = low.astype(f32)
    out_ref[...] = tmp_ref[...].T[:96, :96].astype(bf16)


def stiff_weights(mat_ref, sign, tmp_ref, expand, diag, high_ref, low_ref):
    for d in range(3):
        high, low = split(sign * mat_ref[d])
        tmp_ref[0:BASIS, 32 * d : 32 * d + BASIS] = high.astype(f32)
        tmp_ref[24 : 24 + BASIS, 32 * d : 32 * d + BASIS] = low.astype(f32)
    high_ref[...] = kron8(tmp_ref[0:BASIS, 0:96], expand, diag)
    low_ref[...] = kron8(tmp_ref[24 : 24 + BASIS, 0:96], expand, diag)


def project_weights(proj_ref, tmp_ref, expand, diag, out_ref, packed_ref):
    for f in range(4):
        lay(tmp_ref, 16 * f, proj_ref[:, f, :])
    for f in range(4):
        out_ref[80 * f : 80 * f + 80] = kron8(tmp_ref[16 * f : 16 * f + FACE, 0:96], expand, diag)
    row = iota((128, 64), 0)
    inner = row & 31
    pick = ones_where((inner < 30) & ((row >> 5) * 16 + third(inner) == iota((128, 64), 1)))
    rows = dot(pick, tmp_ref[0:64, 0:96].astype(bf16)).astype(bf16)
    inner = iota((128, 480), 0) & 31
    same = inner - 3 * third(inner) == (iota((128, 480), 1) & 7)
    packed_ref[...] = jnp.where(same, dot(rows, expand), 0.0).astype(bf16)


def rotate_weights(rot_ref, tmp_ref, expand, diag, out_ref, packed_ref):
    for o in range(3):
        lay(tmp_ref, 16 * o, rot_ref[:, o, :])
    row, col = iota((96, 96), 0), iota((96, 96), 1)
    inner = col & 31
    packed = ones_where((inner < 30) & (row >> 5 == col >> 5) & ((row & 31) == third(inner)))
    inner = iota((8, 96), 1) & 31
    same = (inner - 3 * third(inner) == iota((8, 96), 0))[None]
    for o in range(3):
        rows = tmp_ref[16 * o : 16 * o + FACE, 0:96]
        out_ref[80 * o : 80 * o + 80] = kron8(rows, expand, diag)
        packed_ref[80 * o : 80 * o + 80] = kron8(rows, packed, same)


def lift_weights(lift_ref, turn_ref, tmp_ref, expand, diag, out_ref):
    turn_ref[...] = jnp.zeros((128, 128), f32)
    for f in range(4):
        turn_ref[16 * f : 16 * f + FACE, 0:BASIS] = lift_ref[:, f, :]
    lifts = turn_ref[...].T
    for f in range(4):
        lay(tmp_ref, 24 * f, -lifts[0:BASIS, 16 * f : 16 * f + FACE])
    for f in range(4):
        out_ref[f] = kron8(tmp_ref[24 * f : 24 * f + BASIS, 0:96], expand, diag)


def mixed(field, geo, weights):
    high, low = split(field)
    moved = dot(weights, jnp.concatenate([high, low, high], axis=0))
    n = field.shape[1]
    parts = [moved[32 * j : 32 * j + 32].reshape(4, 8, n) for j in range(3)]
    return [
        (geo[d][0] * parts[0] + geo[d][1] * parts[1] + geo[d][2] * parts[2]).reshape(32, n)
        for d in range(3)
    ]


def mix_steps(load, geo, jac_ref, mix_ref):
    def step(b):
        first, second = (mixed(load(b + i), geo, jac_ref[...]) for i in range(2))
        for d in range(3):
            for s in range(4):
                rows = slice(8 * s, 8 * s + 8)
                high, low = split(jnp.concatenate([first[d][rows], second[d][rows]], axis=0))
                at = (d * BASIS + b) * 8
                mix_ref[s, at : at + 16, :] = high
                mix_ref[s, 480 + at : 480 + at + 16, :] = low

    return [functools.partial(step, b) for b in range(0, BASIS, 2)]


def stiff_steps(mix_ref, weights_ref, low_ref, store):
    def step(s):
        high, low = mix_ref[s, :480], mix_ref[s, 480:]
        store(s, dot(weights_ref[...], high) + dot(weights_ref[...], low) + dot(low_ref[...], high))

    return [functools.partial(step, s) for s in range(4)]


def run(*phases):
    for phase in phases:
        for step in phase:
            step()


def kernel(
    remote,
    state_hbm,
    geo_ref,
    nrm_ref,
    speed_ref,
    cluster_ref,
    nbi_ref,
    nbf_ref,
    orient_ref,
    exs_ref,
    exd_ref,
    exz_ref,
    stiff_ref,
    vol_ref,
    jac_ref,
    proj_ref,
    lift_ref,
    rot_ref,
    out_ref,
    state_ref,
    field_a,
    field_b,
    integral_a,
    integral_b,
    mix_a,
    mix_b,
    times,
    own,
    total,
    mine,
    pool,
    ship,
    near,
    cols_v,
    cols_s,
    exp_v,
    exp_s,
    t0,
    t1,
    t2,
    t3,
    t4,
    t5,
    t6,
    w_expand,
    w_jac,
    w_stiff_h,
    w_stiff_l,
    w_vol_h,
    w_vol_l,
    w_proj,
    w_proj3,
    w_rot,
    w_rot3,
    w_lift,
    cols_sem,
    send_sem,
    recv_sem,
):
    fields, integrals, mixes = (field_a, field_b), (integral_a, integral_b), (mix_a, mix_b)
    tmps = (t0, t1, t2, t3, t4, t5, t6)
    halves = range(ELEM // WIDE)

    links = []
    for at, (axis, first, rows) in enumerate(LINKS):
        step = -1 if at % 2 == 0 else 1
        if remote:
            pos, count = lax.axis_index(axis), lax.axis_size(axis)
            there = pos > 0 if step < 0 else pos < count - 1
            target = jnp.clip(pos + step, 0, count - 1)
        else:
            there, target = True, None
        land = first + rows if step < 0 else first - rows
        links.append((axis, there, target, first, land, rows))

    if remote:
        barrier = pltpu.get_barrier_semaphore()
        greeted = 0
        for axis, there, target, *_ in links:

            @pl.when(there)
            def _(axis=axis, target=target):
                pl.semaphore_signal(barrier, inc=1, device_id={axis: target}, device_id_type=MESH)

            greeted = greeted + there.astype(i32)

    state_copy = pltpu.make_async_copy(state_hbm, state_ref, cols_sem.at[2])
    state_copy.start()

    index = nbi_ref[...]
    slots = ROWS * jnp.where(index < ELEM, nbf_ref[...] * ELEM + index, 3 * ELEM + index)
    for t in range(ELEM // 128):
        cols_v[:, t, :] = slots[:, 128 * t : 128 * t + 128]
    exp_v[:, 0:256] = ROWS * exs_ref[...]
    exp_v[:, 256:384] = ROWS * exd_ref[...]
    exp_v[:, 384:512] = ROWS * exz_ref[...]
    index_copies = [
        pltpu.make_async_copy(cols_v, cols_s, cols_sem.at[0]),
        pltpu.make_async_copy(exp_v, exp_s, cols_sem.at[1]),
    ]
    for copy in index_copies:
        copy.start()

    expand20, diag20 = expander(BASIS), diagonal(24 * BASIS)
    for ref in tmps:
        ref[...] = jnp.zeros((128, 128), f32)
    jacobian_weights(jac_ref, tmps[0], w_jac)
    stiff_weights(stiff_ref, -1.0, tmps[1], expand20, diag20, w_stiff_h, w_stiff_l)
    project_weights(proj_ref, tmps[2], expand20, diag20, w_proj, w_proj3)
    w_expand[...] = expand20

    zeros5 = jnp.zeros((5, WIDE), f32)

    def columns(h):
        return slice(h * WIDE, h * WIDE + WIDE)

    def geometry(h):
        return [
            [jnp.broadcast_to(geo_ref[d, j : j + 1, columns(h)], (8, WIDE))[None] for j in range(3)]
            for d in range(3)
        ]

    fine = cluster_ref[...] == 0
    for degree in range(ORDER):
        base = TIME_STEP ** (degree + 1) / math.factorial(degree + 1)
        coarse = base * (2.0 ** (degree + 1) - 1.0)
        times[degree] = jnp.broadcast_to(jnp.where(fine, f32(base), f32(coarse)), (8, ELEM))

    state_copy.wait()
    for h in halves:
        for b in range(BASIS):
            value = jnp.concatenate([state_ref[b, :, columns(h)], zeros5], axis=0)
            fields[h][b] = value
            integrals[h][b] = (times[0, :, columns(h)][None] * value.reshape(4, 8, WIDE)).reshape(32, WIDE)

    def predict(degree, carry):
        phases = [mix_steps(lambda b, h=h: fields[h][b], geometry(h), w_jac, mixes[h]) for h in halves]
        for h in halves:

            def store(s, value, h=h):
                value = value.reshape(BASIS, 8, WIDE)
                rows = slice(8 * s, 8 * s + 8)
                fields[h][:, rows, :] = value
                integrals[h][:, rows, :] += times[degree, :, columns(h)][None] * value

            phases.append(stiff_steps(mixes[h], w_stiff_h, w_stiff_l, store))
        run(*phases)
        return carry

    lax.fori_loop(1, ORDER, predict, 0)

    for h in halves:
        for s in range(4):
            high, low = split(integrals[h][:, 8 * s : 8 * s + 8, :].reshape(BASIS * 8, WIDE))
            operand = jnp.concatenate([high, low, high], axis=0)
            traces = dot(w_proj[...], operand)
            for f in range(4):
                own[f, :, 8 * s : 8 * s + 8, columns(h)] = traces[80 * f : 80 * f + 80].reshape(FACE, 8, WIDE)
            if s == 3:
                packed = dot(w_proj3[...], operand)
        for f in range(4):
            pieces = [own[f, :, 8 * s : 8 * s + 8, columns(h)].reshape(80, WIDE) for s in range(3)]
            whole = jnp.concatenate(pieces + [packed[32 * f : 32 * f + 32]], axis=0)
            for t in range(WIDE // 128):
                base = ROWS * (f * ELEM + h * WIDE + 128 * t)
                for c in range(ROWS):
                    chunk = whole[128 * c : min(128 * c + 128, TRACE), 128 * t : 128 * t + 128]
                    if c == ROWS - 1:
                        chunk = jnp.concatenate([chunk, jnp.zeros((128 - chunk.shape[0], 128), f32)], axis=0)
                    mine[pl.ds(base + c, 128, stride=ROWS), :] = chunk.T

    own_copy = pltpu.make_async_copy(mine, pool.at[pl.ds(0, ROWS * 4 * ELEM), :], cols_sem.at[3])
    own_copy.start()
    for copy in index_copies:
        copy.wait()
    if remote:
        pl.semaphore_wait(barrier, greeted)

    copies = []
    for at, (axis, there, target, first, land, rows) in enumerate(links):
        side = at % 2
        lane = (0, 256, 384)[at // 2]

        for n in range(rows):
            row = exp_s[side, lane + n]
            ship[pl.ds(ROWS * (first + n), ROWS), :] = mine[pl.ds(row, ROWS), :]
        source = ship.at[pl.ds(ROWS * first, ROWS * rows), :]
        goal = pool.at[pl.ds(ROWS * (4 * ELEM + land), ROWS * rows), :]
        if remote:
            copy = pltpu.make_async_remote_copy(
                src_ref=source,
                dst_ref=goal,
                send_sem=send_sem.at[at],
                recv_sem=recv_sem.at[at ^ 1],
                device_id={axis: target},
                device_id_type=MESH,
            )
            pl.when(there)(copy.start)
        else:
            copy = pltpu.make_async_copy(source, goal, send_sem.at[at])
            copy.start()
        copies.append(copy)

    stiff_weights(vol_ref, 1.0, tmps[3], w_expand[...], diag20, w_vol_h, w_vol_l)
    expand10, diag10 = expander(FACE), diagonal(24 * FACE)
    rotate_weights(rot_ref, tmps[4], expand10, diag10, w_rot, w_rot3)
    lift_weights(lift_ref, tmps[6], tmps[5], expand10, diag10, w_lift)

    phases = [mix_steps(lambda b, h=h: integrals[h][b], geometry(h), w_jac, mixes[h]) for h in halves]
    for h in halves:

        def store(s, value, h=h):
            total[s, :, columns(h)] = value

        phases.append(stiff_steps(mixes[h], w_vol_h, w_vol_l, store))
    run(*phases)

    own_copy.wait()
    for at, (axis, there, target, first, land, rows) in enumerate(links):
        copy = copies[at]
        if remote:
            arrived = pltpu.make_async_remote_copy(
                src_ref=ship.at[pl.ds(ROWS * first, ROWS * rows), :],
                dst_ref=pool.at[pl.ds(ROWS * (4 * ELEM + first), ROWS * rows), :],
                send_sem=send_sem.at[at],
                recv_sem=recv_sem.at[at],
                device_id={axis: target},
                device_id_type=MESH,
            )

            @pl.when(there)
            def _(copy=copy, arrived=arrived):
                copy.wait_send()
                arrived.wait_recv()
        else:
            copy.wait()

    def fetch(f, first, count):
        for n in range(first, first + count):
            near[pl.ds(ROWS * n, ROWS), :] = pool[pl.ds(cols_s[f, n // 128, n % 128], ROWS), :]

    def turned(f, h):
        tiles = []
        for t in range(WIDE // 128):
            base = ROWS * (h * WIDE + 128 * t)
            parts = [near[pl.ds(base + c, 128, stride=ROWS), :].T for c in range(ROWS)]
            tiles.append(jnp.concatenate([parts[0], parts[1], parts[2][: TRACE - 256]], axis=0))
        high, low = split(jnp.concatenate(tiles, axis=1))
        turn = jnp.broadcast_to(orient_ref[pl.ds(f, 1), columns(h)], (8, WIDE))[None]
        slabs = []
        for s in range(4):
            rows = slice(80 * s, min(80 * s + 80, TRACE))
            operand = jnp.concatenate([high[rows], low[rows], high[rows]], axis=0)
            ways = dot(w_rot[...] if s < 3 else w_rot3[...], operand).reshape(3, FACE, 8, WIDE)
            slabs.append(jnp.where(turn == 0, ways[0], jnp.where(turn == 1, ways[1], ways[2])))
        return slabs

    def fluxes(f, h, slabs):
        normal = [
            0.5 * jnp.broadcast_to(nrm_ref[j, pl.ds(f, 1), columns(h)], (8, WIDE))[None] for j in range(3)
        ]
        speed = 0.5 * jnp.broadcast_to(speed_ref[:, columns(h)], (8, WIDE))[None]
        flux = []
        for i in range(FACE):
            there = jnp.stack([slabs[s][i] for s in range(4)])
            here = own[f, i, :, columns(h)].reshape(4, 8, WIDE)
            high, low = split((here + there).reshape(32, WIDE))
            moved = dot(w_jac[...], jnp.concatenate([high, low, high], axis=0))
            value = speed * (here - there)
            for j in range(3):
                value = value + normal[j] * moved[32 * j : 32 * j + 32].reshape(4, 8, WIDE)
            flux.append(value)
        return flux

    def lifted(f, h, flux):
        for s in range(4):
            high, low = split(jnp.concatenate([flux[i][s] for i in range(FACE)], axis=0))
            operand = jnp.concatenate([high, low, high], axis=0)
            total[s, :, columns(h)] += dot(w_lift[f], operand)

    fetch(0, 0, ELEM)

    def faces(f, carry):
        later = jnp.minimum(f + 1, 3)
        slabs = [turned(f, h) for h in halves]
        flux = []
        for h in halves:
            flux.append(fluxes(f, h, slabs[h]))
            fetch(later, h * (ELEM // 4), ELEM // 4)
        for h in halves:
            lifted(f, h, flux[h])
            fetch(later, ELEM // 2 + h * (ELEM // 4), ELEM // 4)
        return carry

    lax.fori_loop(0, 4, faces, 0)

    for h in halves:
        keep = jnp.broadcast_to(cluster_ref[:, columns(h)], (8, WIDE)) == 0
        for b in range(BASIS):
            for s in range(4):
                n = min(8, QUANT - 8 * s)
                update = jnp.where(keep, total[s, 8 * b : 8 * b + 8, columns(h)], 0.0)[:n]
                out_ref[b, 8 * s : 8 * s + n, columns(h)] = (
                    state_ref[b, 8 * s : 8 * s + n, columns(h)] + update
                )


def update_call(remote, *args):
    vmem = pl.BlockSpec(memory_space=pltpu.VMEM)
    return pl.pallas_call(
        functools.partial(kernel, remote),
        out_shape=pltpu.VMEM((BASIS, QUANT, ELEM), f32),
        in_specs=[pl.BlockSpec(memory_space=pl.ANY)] + [vmem] * 16,
        out_specs=vmem,
        scratch_shapes=[
            pltpu.VMEM((BASIS, QUANT, ELEM), f32),
            pltpu.VMEM((BASIS, 32, WIDE), f32),
            pltpu.VMEM((BASIS, 32, WIDE), f32),
            pltpu.VMEM((BASIS, 32, WIDE), f32),
            pltpu.VMEM((BASIS, 32, WIDE), f32),
            pltpu.VMEM((4, 960, WIDE), bf16),
            pltpu.VMEM((4, 960, WIDE), bf16),
            pltpu.VMEM((ORDER, 8, ELEM), f32),
            pltpu.VMEM((4, FACE, 32, ELEM), f32),
            pltpu.VMEM((4, 160, ELEM), f32),
            pltpu.VMEM((ROWS * 4 * ELEM, 128), f32),
            pltpu.VMEM((ROWS * 6 * ELEM, 128), f32),
            pltpu.VMEM((ROWS * 2 * ELEM, 128), f32),
            pltpu.VMEM((ROWS * ELEM, 128), f32),
            pltpu.VMEM((4, 4, 128), i32),
            pltpu.SMEM((4, 4, 128), i32),
            pltpu.VMEM((2, ELEM), i32),
            pltpu.SMEM((2, ELEM), i32),
            *[pltpu.VMEM((128, 128), f32)] * 7,
            pltpu.VMEM((96, 480), bf16),
            pltpu.VMEM((96, 96), bf16),
            pltpu.VMEM((160, 480), bf16),
            pltpu.VMEM((160, 480), bf16),
            pltpu.VMEM((160, 480), bf16),
            pltpu.VMEM((160, 480), bf16),
            pltpu.VMEM((320, 480), bf16),
            pltpu.VMEM((128, 480), bf16),
            pltpu.VMEM((240, 240), bf16),
            pltpu.VMEM((240, 96), bf16),
            pltpu.VMEM((4, 160, 240), bf16),
            pltpu.SemaphoreType.DMA((4,)),
            pltpu.SemaphoreType.DMA((6,)),
            pltpu.SemaphoreType.DMA((6,)),
        ],
        compiler_params=pltpu.CompilerParams(
            vmem_limit_bytes=56 * 2**20,
            **(dict(collective_id=0, has_side_effects=True) if remote else {}),
        ),
    )(*args)


def arranged(args):
    state, geometry, normals, speed, cluster, *rest, proj, lift, rot = args
    return (
        state,
        geometry,
        jnp.transpose(normals, (1, 0, 2)),
        speed.reshape(1, ELEM),
        cluster.reshape(1, ELEM),
        *rest,
        jnp.transpose(proj, (1, 0, 2)),
        jnp.transpose(lift, (2, 0, 1)),
        jnp.transpose(rot, (1, 0, 2)),
    )


def per_device(*args):
    return update_call(True, *arranged(args))


def solution(mesh):
    whole = ("strike", "dip", "depth")
    placed = (
        (P(None, None, whole),) * 3 + (P(whole),) * 2 + (P(None, whole),) * 6 + (P(),) * 6
    )
    return jax.shard_map(
        per_device,
        mesh=mesh,
        in_specs=placed,
        out_specs=P(None, None, whole),
        check_vma=False,
    )
```

```python
import functools
import math

import jax
import jax.numpy as jnp
from jax import lax
from jax.experimental import pallas as pl
from jax.experimental.pallas import tpu as pltpu
from jax.sharding import PartitionSpec as P

MESH = pl.DeviceIdType.MESH
BASIS, QUANT, FACE = 20, 27, 10
ELEM = 512
TIME_STEP = 0.5
ORDER = 4
WIDE = 256
ROWS = 3
TRACE = 272
f32, bf16, i32 = jnp.float32, jnp.bfloat16, jnp.int32

LINKS = (
    ("strike", -1, 0, 256, 128),
    ("strike", 1, 256, 0, 128),
    ("dip", -1, 512, 640, 128),
    ("dip", 1, 640, 512, 128),
    ("depth", -1, 768, 896, 128),
    ("depth", 1, 896, 768, 128),
    ("strike", -1, 128, 384, 128),
    ("strike", 1, 384, 128, 128),
)
LANES = {"strike": 0, "dip": 256, "depth": 384}
STARTS = {"strike": 0, "dip": 512, "depth": 768}
WIDTHS = {"strike": 256, "dip": 128, "depth": 128}


def dot(a, b):
    return jnp.dot(a, b, preferred_element_type=f32)


def split(x):
    high = x.astype(bf16)
    return high, (x - high.astype(f32)).astype(bf16)


def rep8(m):
    n, k = m.shape
    return jnp.broadcast_to(m[:, None, :], (n, 8, k)).reshape(n * 8, k)


def iota(shape, dim):
    return lax.broadcasted_iota(i32, shape, dim)


def ones_where(mask):
    return jnp.where(mask, 1.0, 0.0).astype(bf16)


def expander(count):
    shape = (96, 24 * count)
    row, entry = iota(shape, 0), iota(shape, 1) >> 3
    part = row >> 5
    inner = row & 31
    return ones_where((inner < count) & (entry == part * count + inner))


def diagonal(width):
    return (iota((8, width), 0) == (iota((8, width), 1) & 7))[None]


def kron8(rows, expand, diag):
    n, width = rows.shape[0], expand.shape[1]
    wide = dot(rep8(rows).astype(bf16), expand).reshape(n, 8, width)
    return jnp.where(diag, wide, 0.0).reshape(n * 8, width).astype(bf16)


def lay(tmp_ref, at, m):
    n, k = m.shape
    high, low = (piece.astype(f32) for piece in split(m))
    for part, piece in enumerate((high, high, low)):
        tmp_ref[at : at + n, 32 * part : 32 * part + k] = piece


def third(x):
    return (x * 171) >> 9


def jacobian_weights(jac_ref, tmp_ref, out_ref):
    for j in range(3):
        high, low = split(jac_ref[j])
        at = slice(32 * j, 32 * j + QUANT)
        tmp_ref[0:QUANT, at] = high.astype(f32)
        tmp_ref[32 : 32 + QUANT, at] = high.astype(f32)
        tmp_ref[64 : 64 + QUANT, at] = low.astype(f32)
    out_ref[...] = tmp_ref[...].T[:96, :96].astype(bf16)


def stiff_weights(mat_ref, sign, tmp_ref, expand, diag, high_ref, low_ref):
    for d in range(3):
        high, low = split(sign * mat_ref[d])
        tmp_ref[0:BASIS, 32 * d : 32 * d + BASIS] = high.astype(f32)
        tmp_ref[24 : 24 + BASIS, 32 * d : 32 * d + BASIS] = low.astype(f32)
    high_ref[...] = kron8(tmp_ref[0:BASIS, 0:96], expand, diag)
    low_ref[...] = kron8(tmp_ref[24 : 24 + BASIS, 0:96], expand, diag)


def project_weights(proj_ref, tmp_ref, expand, diag, out_ref, packed_ref):
    for f in range(4):
        lay(tmp_ref, 16 * f, proj_ref[:, f, :])
    for f in range(4):
        out_ref[80 * f : 80 * f + 80] = kron8(tmp_ref[16 * f : 16 * f + FACE, 0:96], expand, diag)
    row = iota((128, 64), 0)
    inner = row & 31
    pick = ones_where((inner < 30) & ((row >> 5) * 16 + third(inner) == iota((128, 64), 1)))
    rows = dot(pick, tmp_ref[0:64, 0:96].astype(bf16)).astype(bf16)
    inner = iota((128, 480), 0) & 31
    same = inner - 3 * third(inner) == (iota((128, 480), 1) & 7)
    packed_ref[...] = jnp.where(same, dot(rows, expand), 0.0).astype(bf16)


def rotate_weights(rot_ref, tmp_ref, expand, diag, out_ref, packed_ref):
    for o in range(3):
        lay(tmp_ref, 16 * o, rot_ref[:, o, :])
    row, col = iota((96, 96), 0), iota((96, 96), 1)
    inner = col & 31
    packed = ones_where((inner < 30) & (row >> 5 == col >> 5) & ((row & 31) == third(inner)))
    inner = iota((8, 96), 1) & 31
    same = (inner - 3 * third(inner) == iota((8, 96), 0))[None]
    for o in range(3):
        rows = tmp_ref[16 * o : 16 * o + FACE, 0:96]
        out_ref[80 * o : 80 * o + 80] = kron8(rows, expand, diag)
        packed_ref[80 * o : 80 * o + 80] = kron8(rows, packed, same)


def lift_weights(lift_ref, turn_ref, tmp_ref, expand, diag, out_ref):
    turn_ref[...] = jnp.zeros((128, 128), f32)
    for f in range(4):
        turn_ref[16 * f : 16 * f + FACE, 0:BASIS] = lift_ref[:, f, :]
    lifts = turn_ref[...].T
    for f in range(4):
        lay(tmp_ref, 24 * f, -lifts[0:BASIS, 16 * f : 16 * f + FACE])
    for f in range(4):
        out_ref[f] = kron8(tmp_ref[24 * f : 24 * f + BASIS, 0:96], expand, diag)


def mixed(field, geo, weights):
    high, low = split(field)
    moved = dot(weights, jnp.concatenate([high, low, high], axis=0))
    n = field.shape[1]
    parts = [moved[32 * j : 32 * j + 32].reshape(4, 8, n) for j in range(3)]
    return [
        (geo[d][0] * parts[0] + geo[d][1] * parts[1] + geo[d][2] * parts[2]).reshape(32, n)
        for d in range(3)
    ]


def mix_steps(load, geo, jac_ref, mix_ref):
    def step(b):
        first, second = (mixed(load(b + i), geo, jac_ref[...]) for i in range(2))
        for d in range(3):
            for s in range(4):
                rows = slice(8 * s, 8 * s + 8)
                high, low = split(jnp.concatenate([first[d][rows], second[d][rows]], axis=0))
                at = (d * BASIS + b) * 8
                mix_ref[s, at : at + 16, :] = high
                mix_ref[s, 480 + at : 480 + at + 16, :] = low

    return [functools.partial(step, b) for b in range(0, BASIS, 2)]


def stiff_steps(mix_ref, weights_ref, low_ref, store):
    def step(s):
        high, low = mix_ref[s, :480], mix_ref[s, 480:]
        store(s, dot(weights_ref[...], high) + dot(weights_ref[...], low) + dot(low_ref[...], high))

    return [functools.partial(step, s) for s in range(4)]


def run(*phases):
    for phase in phases:
        for step in phase:
            step()


def kernel(
    remote,
    state_hbm,
    geo_ref,
    nrm_ref,
    speed_ref,
    cluster_ref,
    nbi_ref,
    nbf_ref,
    orient_ref,
    exs_ref,
    exd_ref,
    exz_ref,
    stiff_ref,
    vol_ref,
    jac_ref,
    proj_ref,
    lift_ref,
    rot_ref,
    out_ref,
    state_ref,
    field_a,
    field_b,
    integral_a,
    integral_b,
    mix_a,
    mix_b,
    times,
    own,
    total,
    mine,
    pool,
    ship,
    near,
    cols_v,
    cols_s,
    exp_v,
    exp_s,
    t0,
    t1,
    t2,
    t3,
    t4,
    t5,
    t6,
    w_expand,
    w_jac,
    w_stiff_h,
    w_stiff_l,
    w_vol_h,
    w_vol_l,
    w_proj,
    w_proj3,
    w_rot,
    w_rot3,
    w_lift,
    cols_sem,
    send_sem,
    recv_sem,
):
    fields, integrals, mixes = (field_a, field_b), (integral_a, integral_b), (mix_a, mix_b)
    tmps = (t0, t1, t2, t3, t4, t5, t6)
    halves = range(ELEM // WIDE)

    sides = {}
    for axis in ("strike", "dip", "depth"):
        for step in (-1, 1):
            if remote:
                pos, count = lax.axis_index(axis), lax.axis_size(axis)
                there = pos > 0 if step < 0 else pos < count - 1
                sides[axis, step] = there, jnp.clip(pos + step, 0, count - 1)
            else:
                sides[axis, step] = True, None

    if remote:
        barrier = pltpu.get_barrier_semaphore()
        greeted = 0
        for (axis, step), (there, target) in sides.items():

            @pl.when(there)
            def _(axis=axis, target=target):
                pl.semaphore_signal(barrier, inc=1, device_id={axis: target}, device_id_type=MESH)

            greeted = greeted + there.astype(i32)

    state_copy = pltpu.make_async_copy(state_hbm, state_ref, cols_sem.at[2])
    state_copy.start()

    index = nbi_ref[...]
    slots = ROWS * jnp.where(index < ELEM, nbf_ref[...] * ELEM + index, 3 * ELEM + index)
    for t in range(ELEM // 128):
        cols_v[:, t, :] = slots[:, 128 * t : 128 * t + 128]
    exp_v[:, 0:256] = ROWS * exs_ref[...]
    exp_v[:, 256:384] = ROWS * exd_ref[...]
    exp_v[:, 384:512] = ROWS * exz_ref[...]
    index_copies = [
        pltpu.make_async_copy(cols_v, cols_s, cols_sem.at[0]),
        pltpu.make_async_copy(exp_v, exp_s, cols_sem.at[1]),
    ]
    for copy in index_copies:
        copy.start()

    expand20, diag20 = expander(BASIS), diagonal(24 * BASIS)
    for ref in tmps:
        ref[...] = jnp.zeros((128, 128), f32)
    jacobian_weights(jac_ref, tmps[0], w_jac)
    stiff_weights(stiff_ref, -1.0, tmps[1], expand20, diag20, w_stiff_h, w_stiff_l)
    project_weights(proj_ref, tmps[2], expand20, diag20, w_proj, w_proj3)
    w_expand[...] = expand20

    zeros5 = jnp.zeros((5, WIDE), f32)

    def columns(h):
        return slice(h * WIDE, h * WIDE + WIDE)

    def geometry(h):
        return [
            [jnp.broadcast_to(geo_ref[d, j : j + 1, columns(h)], (8, WIDE))[None] for j in range(3)]
            for d in range(3)
        ]

    fine = cluster_ref[...] == 0
    for degree in range(ORDER):
        base = TIME_STEP ** (degree + 1) / math.factorial(degree + 1)
        coarse = base * (2.0 ** (degree + 1) - 1.0)
        times[degree] = jnp.broadcast_to(jnp.where(fine, f32(base), f32(coarse)), (8, ELEM))

    state_copy.wait()
    for h in halves:
        for b in range(BASIS):
            value = jnp.concatenate([state_ref[b, :, columns(h)], zeros5], axis=0)
            fields[h][b] = value
            integrals[h][b] = (times[0, :, columns(h)][None] * value.reshape(4, 8, WIDE)).reshape(32, WIDE)

    def predict(degree, carry):
        phases = [mix_steps(lambda b, h=h: fields[h][b], geometry(h), w_jac, mixes[h]) for h in halves]
        for h in halves:

            def store(s, value, h=h):
                value = value.reshape(BASIS, 8, WIDE)
                rows = slice(8 * s, 8 * s + 8)
                fields[h][:, rows, :] = value
                integrals[h][:, rows, :] += times[degree, :, columns(h)][None] * value

            phases.append(stiff_steps(mixes[h], w_stiff_h, w_stiff_l, store))
        run(*phases)
        return carry

    lax.fori_loop(1, ORDER, predict, 0)

    def operand(h, s):
        high, low = split(integrals[h][:, 8 * s : 8 * s + 8, :].reshape(BASIS * 8, WIDE))
        return jnp.concatenate([high, low, high], axis=0)

    def keep_own(f, h, s, rows):
        own[f, :, 8 * s : 8 * s + 8, columns(h)] = rows.reshape(FACE, 8, WIDE)

    for h in halves:
        operands = [operand(h, s) for s in range(4)]
        packed = dot(w_proj3[...], operands[3])
        for pair in (0, 2):
            slabs = [dot(w_proj[80 * pair : 80 * pair + 160], operands[s]) for s in range(3)]
            for f in (pair, pair + 1):
                pieces = [slab[80 * (f - pair) : 80 * (f - pair) + 80] for slab in slabs]
                for s in range(3):
                    keep_own(f, h, s, pieces[s])
                whole = jnp.concatenate(pieces + [packed[32 * f : 32 * f + 32]], axis=0)
                for t in range(WIDE // 128):
                    base = ROWS * (f * ELEM + h * WIDE + 128 * t)
                    for c in range(ROWS):
                        chunk = whole[128 * c : min(128 * c + 128, TRACE), 128 * t : 128 * t + 128]
                        if c == ROWS - 1:
                            short = jnp.zeros((128 - chunk.shape[0], 128), f32)
                            chunk = jnp.concatenate([chunk, short], axis=0)
                        mine[pl.ds(base + c, 128, stride=ROWS), :] = chunk.T

    own_copy = pltpu.make_async_copy(mine, pool.at[pl.ds(0, ROWS * 4 * ELEM), :], cols_sem.at[3])
    own_copy.start()
    for copy in index_copies:
        copy.wait()
    if remote:
        pl.semaphore_wait(barrier, greeted)

    def link(at):
        axis, step, first, land, rows = LINKS[at]
        source = ship.at[pl.ds(ROWS * first, ROWS * rows), :]
        goal = pool.at[pl.ds(ROWS * (4 * ELEM + land), ROWS * rows), :]
        if not remote:
            return pltpu.make_async_copy(source, goal, send_sem.at[at])
        return pltpu.make_async_remote_copy(
            src_ref=source,
            dst_ref=goal,
            send_sem=send_sem.at[at],
            recv_sem=recv_sem.at[at],
            device_id={axis: sides[axis, step][1]},
            device_id_type=MESH,
        )

    for at, (axis, step, first, land, rows) in enumerate(LINKS):
        side = 0 if step < 0 else 1
        lane = LANES[axis] + first - STARTS[axis] - side * WIDTHS[axis]
        for n in range(rows):
            row = exp_s[side, lane + n]
            ship[pl.ds(ROWS * (first + n), ROWS), :] = mine[pl.ds(row, ROWS), :]
        if remote:
            pl.when(sides[axis, step][0])(link(at).start)
        else:
            link(at).start()

    for h in halves:
        rows = dot(w_proj[...], operand(h, 3))
        for f in range(4):
            keep_own(f, h, 3, rows[80 * f : 80 * f + 80])
    stiff_weights(vol_ref, 1.0, tmps[3], w_expand[...], diag20, w_vol_h, w_vol_l)
    expand10, diag10 = expander(FACE), diagonal(24 * FACE)
    rotate_weights(rot_ref, tmps[4], expand10, diag10, w_rot, w_rot3)
    lift_weights(lift_ref, tmps[6], tmps[5], expand10, diag10, w_lift)

    phases = [mix_steps(lambda b, h=h: integrals[h][b], geometry(h), w_jac, mixes[h]) for h in halves]
    for h in halves:

        def store(s, value, h=h):
            total[s, :, columns(h)] = value

        phases.append(stiff_steps(mixes[h], w_vol_h, w_vol_l, store))
    run(*phases)

    own_copy.wait()
    for at, (axis, step, *_) in enumerate(LINKS):
        copy = link(at)
        if remote:
            pl.when(sides[axis, step][0])(copy.wait_send)
            pl.when(sides[axis, -step][0])(copy.wait_recv)
        else:
            copy.wait()

    def fetch(f, first, count):
        for n in range(first, first + count):
            near[pl.ds(ROWS * n, ROWS), :] = pool[pl.ds(cols_s[f, n // 128, n % 128], ROWS), :]

    def turned(f, h):
        tiles = []
        for t in range(WIDE // 128):
            base = ROWS * (h * WIDE + 128 * t)
            parts = [near[pl.ds(base + c, 128, stride=ROWS), :].T for c in range(ROWS)]
            tiles.append(jnp.concatenate([parts[0], parts[1], parts[2][: TRACE - 256]], axis=0))
        high, low = split(jnp.concatenate(tiles, axis=1))
        turn = jnp.broadcast_to(orient_ref[f : f + 1, columns(h)], (8, WIDE))[None]
        slabs = []
        for s in range(4):
            rows = slice(80 * s, min(80 * s + 80, TRACE))
            operand = jnp.concatenate([high[rows], low[rows], high[rows]], axis=0)
            ways = dot(w_rot[...] if s < 3 else w_rot3[...], operand).reshape(3, FACE, 8, WIDE)
            slabs.append(jnp.where(turn == 0, ways[0], jnp.where(turn == 1, ways[1], ways[2])))
        return slabs

    def fluxes(f, h, slabs):
        normal = [
            0.5 * jnp.broadcast_to(nrm_ref[j, f : f + 1, columns(h)], (8, WIDE))[None] for j in range(3)
        ]
        speed = 0.5 * jnp.broadcast_to(speed_ref[:, columns(h)], (8, WIDE))[None]
        flux = []
        for i in range(FACE):
            there = jnp.stack([slabs[s][i] for s in range(4)])
            here = own[f, i, :, columns(h)].reshape(4, 8, WIDE)
            high, low = split((here + there).reshape(32, WIDE))
            moved = dot(w_jac[...], jnp.concatenate([high, low, high], axis=0))
            value = speed * (here - there)
            for j in range(3):
                value = value + normal[j] * moved[32 * j : 32 * j + 32].reshape(4, 8, WIDE)
            flux.append(value)
        return flux

    def lifted(f, h, flux):
        for s in range(4):
            high, low = split(jnp.concatenate([flux[i][s] for i in range(FACE)], axis=0))
            operand = jnp.concatenate([high, low, high], axis=0)
            total[s, :, columns(h)] += dot(w_lift[f], operand)

    fetch(0, 0, ELEM)
    slabs = [turned(0, h) for h in halves]
    fetch(1, 0, ELEM)
    for f in range(4):
        flux, later = [], []
        for h in halves:
            if f < 3:
                later.append(turned(f + 1, h))
            flux.append(fluxes(f, h, slabs[h]))
        for h in halves:
            lifted(f, h, flux[h])
            if f < 2:
                fetch(f + 2, h * (ELEM // 2), ELEM // 2)
        slabs = later

    for h in halves:
        keep = jnp.broadcast_to(cluster_ref[:, columns(h)], (8, WIDE)) == 0
        for b in range(BASIS):
            for s in range(4):
                n = min(8, QUANT - 8 * s)
                update = jnp.where(keep, total[s, 8 * b : 8 * b + 8, columns(h)], 0.0)[:n]
                out_ref[b, 8 * s : 8 * s + n, columns(h)] = (
                    state_ref[b, 8 * s : 8 * s + n, columns(h)] + update
                )


def update_call(remote, *args):
    vmem = pl.BlockSpec(memory_space=pltpu.VMEM)
    return pl.pallas_call(
        functools.partial(kernel, remote),
        out_shape=pltpu.VMEM((BASIS, QUANT, ELEM), f32),
        in_specs=[pl.BlockSpec(memory_space=pl.ANY)] + [vmem] * 16,
        out_specs=vmem,
        scratch_shapes=[
            pltpu.VMEM((BASIS, QUANT, ELEM), f32),
            pltpu.VMEM((BASIS, 32, WIDE), f32),
            pltpu.VMEM((BASIS, 32, WIDE), f32),
            pltpu.VMEM((BASIS, 32, WIDE), f32),
            pltpu.VMEM((BASIS, 32, WIDE), f32),
            pltpu.VMEM((4, 960, WIDE), bf16),
            pltpu.VMEM((4, 960, WIDE), bf16),
            pltpu.VMEM((ORDER, 8, ELEM), f32),
            pltpu.VMEM((4, FACE, 32, ELEM), f32),
            pltpu.VMEM((4, 160, ELEM), f32),
            pltpu.VMEM((ROWS * 4 * ELEM, 128), f32),
            pltpu.VMEM((ROWS * 6 * ELEM, 128), f32),
            pltpu.VMEM((ROWS * 2 * ELEM, 128), f32),
            pltpu.VMEM((ROWS * ELEM, 128), f32),
            pltpu.VMEM((4, 4, 128), i32),
            pltpu.SMEM((4, 4, 128), i32),
            pltpu.VMEM((2, ELEM), i32),
            pltpu.SMEM((2, ELEM), i32),
            *[pltpu.VMEM((128, 128), f32)] * 7,
            pltpu.VMEM((96, 480), bf16),
            pltpu.VMEM((96, 96), bf16),
            pltpu.VMEM((160, 480), bf16),
            pltpu.VMEM((160, 480), bf16),
            pltpu.VMEM((160, 480), bf16),
            pltpu.VMEM((160, 480), bf16),
            pltpu.VMEM((320, 480), bf16),
            pltpu.VMEM((128, 480), bf16),
            pltpu.VMEM((240, 240), bf16),
            pltpu.VMEM((240, 96), bf16),
            pltpu.VMEM((4, 160, 240), bf16),
            pltpu.SemaphoreType.DMA((4,)),
            pltpu.SemaphoreType.DMA((8,)),
            pltpu.SemaphoreType.DMA((8,)),
        ],
        compiler_params=pltpu.CompilerParams(
            vmem_limit_bytes=56 * 2**20,
            **(dict(collective_id=0, has_side_effects=True) if remote else {}),
        ),
    )(*args)


def arranged(args):
    state, geometry, normals, speed, cluster, *rest, proj, lift, rot = args
    return (
        state,
        geometry,
        jnp.transpose(normals, (1, 0, 2)),
        speed.reshape(1, ELEM),
        cluster.reshape(1, ELEM),
        *rest,
        jnp.transpose(proj, (1, 0, 2)),
        jnp.transpose(lift, (2, 0, 1)),
        jnp.transpose(rot, (1, 0, 2)),
    )


def per_device(*args):
    return update_call(True, *arranged(args))


def solution(mesh):
    whole = ("strike", "dip", "depth")
    placed = (
        (P(None, None, whole),) * 3 + (P(whole),) * 2 + (P(None, whole),) * 6 + (P(),) * 6
    )
    return jax.shard_map(
        per_device,
        mesh=mesh,
        in_specs=placed,
        out_specs=P(None, None, whole),
        check_vma=False,
    )
```

```python
import functools
import math

import jax
import jax.numpy as jnp
from jax import lax
from jax.experimental import pallas as pl
from jax.experimental.pallas import tpu as pltpu
from jax.sharding import PartitionSpec as P

MESH = pl.DeviceIdType.MESH
BASIS, QUANT, FACE = 20, 27, 10
ELEM = 512
TIME_STEP = 0.5
ORDER = 4
WIDE = 256
ROWS = 3
TRACE = 272
LINK = 128
PARCEL = 2 * LINK + LINK // 8
f32, bf16, i32 = jnp.float32, jnp.bfloat16, jnp.int32

LINKS = (
    ("strike", -1, 0, 256),
    ("strike", 1, 256, 0),
    ("dip", -1, 512, 640),
    ("dip", 1, 640, 512),
    ("depth", -1, 768, 896),
    ("depth", 1, 896, 768),
    ("strike", -1, 128, 384),
    ("strike", 1, 384, 128),
)
LANES = {"strike": 0, "dip": 256, "depth": 384}
STARTS = {"strike": 0, "dip": 512, "depth": 768}
WIDTHS = {"strike": 256, "dip": 128, "depth": 128}


def dot(a, b):
    return jnp.dot(a, b, preferred_element_type=f32)


def split(x):
    high = x.astype(bf16)
    return high, (x - high.astype(f32)).astype(bf16)


def rep8(m):
    n, k = m.shape
    return jnp.broadcast_to(m[:, None, :], (n, 8, k)).reshape(n * 8, k)


def iota(shape, dim):
    return lax.broadcasted_iota(i32, shape, dim)


def ones_where(mask):
    return jnp.where(mask, 1.0, 0.0).astype(bf16)


def expander(count):
    shape = (96, 24 * count)
    row, entry = iota(shape, 0), iota(shape, 1) >> 3
    part = row >> 5
    inner = row & 31
    return ones_where((inner < count) & (entry == part * count + inner))


def diagonal(width):
    return (iota((8, width), 0) == (iota((8, width), 1) & 7))[None]


def kron8(rows, expand, diag):
    n, width = rows.shape[0], expand.shape[1]
    wide = dot(rep8(rows).astype(bf16), expand).reshape(n, 8, width)
    return jnp.where(diag, wide, 0.0).reshape(n * 8, width).astype(bf16)


def lay(tmp_ref, at, m):
    n, k = m.shape
    high, low = (piece.astype(f32) for piece in split(m))
    for part, piece in enumerate((high, high, low)):
        tmp_ref[at : at + n, 32 * part : 32 * part + k] = piece


def third(x):
    return (x * 171) >> 9


def jacobian_weights(jac_ref, tmp_ref, out_ref):
    for j in range(3):
        high, low = split(jac_ref[j])
        at = slice(32 * j, 32 * j + QUANT)
        tmp_ref[0:QUANT, at] = high.astype(f32)
        tmp_ref[32 : 32 + QUANT, at] = high.astype(f32)
        tmp_ref[64 : 64 + QUANT, at] = low.astype(f32)
    out_ref[...] = tmp_ref[...].T[:96, :96].astype(bf16)


def stiff_weights(mat_ref, sign, tmp_ref, expand, diag, high_ref, low_ref):
    for d in range(3):
        high, low = split(sign * mat_ref[d])
        tmp_ref[0:BASIS, 32 * d : 32 * d + BASIS] = high.astype(f32)
        tmp_ref[24 : 24 + BASIS, 32 * d : 32 * d + BASIS] = low.astype(f32)
    high_ref[...] = kron8(tmp_ref[0:BASIS, 0:96], expand, diag)
    low_ref[...] = kron8(tmp_ref[24 : 24 + BASIS, 0:96], expand, diag)


def project_weights(proj_ref, tmp_ref, expand, diag, out_ref, packed_ref):
    for f in range(4):
        lay(tmp_ref, 16 * f, proj_ref[:, f, :])
    for f in range(4):
        out_ref[80 * f : 80 * f + 80] = kron8(tmp_ref[16 * f : 16 * f + FACE, 0:96], expand, diag)
    row = iota((128, 64), 0)
    inner = row & 31
    pick = ones_where((inner < 30) & ((row >> 5) * 16 + third(inner) == iota((128, 64), 1)))
    rows = dot(pick, tmp_ref[0:64, 0:96].astype(bf16)).astype(bf16)
    inner = iota((128, 480), 0) & 31
    same = inner - 3 * third(inner) == (iota((128, 480), 1) & 7)
    packed_ref[...] = jnp.where(same, dot(rows, expand), 0.0).astype(bf16)


def rotate_weights(rot_ref, tmp_ref, expand, diag, out_ref, packed_ref):
    for o in range(3):
        lay(tmp_ref, 16 * o, rot_ref[:, o, :])
    row, col = iota((96, 96), 0), iota((96, 96), 1)
    inner = col & 31
    packed = ones_where((inner < 30) & (row >> 5 == col >> 5) & ((row & 31) == third(inner)))
    inner = iota((8, 96), 1) & 31
    same = (inner - 3 * third(inner) == iota((8, 96), 0))[None]
    for o in range(3):
        rows = tmp_ref[16 * o : 16 * o + FACE, 0:96]
        out_ref[80 * o : 80 * o + 80] = kron8(rows, expand, diag)
        packed_ref[80 * o : 80 * o + 80] = kron8(rows, packed, same)


def lift_weights(lift_ref, turn_ref, tmp_ref, expand, diag, out_ref):
    turn_ref[...] = jnp.zeros((128, 128), f32)
    for f in range(4):
        turn_ref[16 * f : 16 * f + FACE, 0:BASIS] = lift_ref[:, f, :]
    lifts = turn_ref[...].T
    for f in range(4):
        lay(tmp_ref, 24 * f, -lifts[0:BASIS, 16 * f : 16 * f + FACE])
    for f in range(4):
        out_ref[f] = kron8(tmp_ref[24 * f : 24 * f + BASIS, 0:96], expand, diag)


def mixed(field, geo, weights):
    high, low = split(field)
    moved = dot(weights, jnp.concatenate([high, low, high], axis=0))
    n = field.shape[1]
    parts = [moved[32 * j : 32 * j + 32].reshape(4, 8, n) for j in range(3)]
    return [
        (geo[d][0] * parts[0] + geo[d][1] * parts[1] + geo[d][2] * parts[2]).reshape(32, n)
        for d in range(3)
    ]


def mix_steps(load, geo, jac_ref, mix_ref):
    def step(b):
        first, second = (mixed(load(b + i), geo, jac_ref[...]) for i in range(2))
        for d in range(3):
            for s in range(4):
                rows = slice(8 * s, 8 * s + 8)
                high, low = split(jnp.concatenate([first[d][rows], second[d][rows]], axis=0))
                at = (d * BASIS + b) * 8
                mix_ref[s, at : at + 16, :] = high
                mix_ref[s, 480 + at : 480 + at + 16, :] = low

    return [functools.partial(step, b) for b in range(0, BASIS, 2)]


def stiff_steps(mix_ref, weights_ref, low_ref, store):
    def step(s):
        high, low = mix_ref[s, :480], mix_ref[s, 480:]
        store(s, dot(weights_ref[...], high) + dot(weights_ref[...], low) + dot(low_ref[...], high))

    return [functools.partial(step, s) for s in range(4)]


def run(*phases):
    for phase in phases:
        for step in phase:
            step()


def kernel(
    remote,
    state_hbm,
    geo_ref,
    nrm_ref,
    speed_ref,
    cluster_ref,
    nbi_ref,
    nbf_ref,
    orient_ref,
    exs_ref,
    exd_ref,
    exz_ref,
    stiff_ref,
    vol_ref,
    jac_ref,
    proj_ref,
    lift_ref,
    rot_ref,
    out_ref,
    state_ref,
    field_a,
    field_b,
    integral_a,
    integral_b,
    mix_a,
    mix_b,
    times,
    own,
    total,
    pool,
    ship,
    thirds,
    arrive,
    near,
    cols_v,
    cols_s,
    exp_v,
    exp_s,
    t0,
    t1,
    t2,
    t3,
    t4,
    t5,
    t6,
    w_expand,
    w_jac,
    w_stiff_h,
    w_stiff_l,
    w_vol_h,
    w_vol_l,
    w_proj,
    w_proj3,
    w_rot,
    w_rot3,
    w_lift,
    cols_sem,
    send_sem,
    recv_sem,
):
    fields, integrals, mixes = (field_a, field_b), (integral_a, integral_b), (mix_a, mix_b)
    tmps = (t0, t1, t2, t3, t4, t5, t6)
    halves = range(ELEM // WIDE)

    sides = {}
    for axis in ("strike", "dip", "depth"):
        for step in (-1, 1):
            if remote:
                pos, count = lax.axis_index(axis), lax.axis_size(axis)
                there = pos > 0 if step < 0 else pos < count - 1
                sides[axis, step] = there, jnp.clip(pos + step, 0, count - 1)
            else:
                sides[axis, step] = True, None

    if remote:
        barrier = pltpu.get_barrier_semaphore()
        greeted = 0
        for (axis, step), (there, target) in sides.items():

            @pl.when(there)
            def _(axis=axis, target=target):
                pl.semaphore_signal(barrier, inc=1, device_id={axis: target}, device_id_type=MESH)

            greeted = greeted + there.astype(i32)

    state_copy = pltpu.make_async_copy(state_hbm, state_ref, cols_sem.at[2])
    state_copy.start()

    index = nbi_ref[...]
    slots = ROWS * jnp.where(index < ELEM, nbf_ref[...] * ELEM + index, 3 * ELEM + index)
    for t in range(ELEM // 128):
        cols_v[:, t, :] = slots[:, 128 * t : 128 * t + 128]
    exp_v[:, 0:256] = ROWS * exs_ref[...]
    exp_v[:, 256:384] = ROWS * exd_ref[...]
    exp_v[:, 384:512] = ROWS * exz_ref[...]
    index_copies = [
        pltpu.make_async_copy(cols_v, cols_s, cols_sem.at[0]),
        pltpu.make_async_copy(exp_v, exp_s, cols_sem.at[1]),
    ]
    for copy in index_copies:
        copy.start()

    expand20, diag20 = expander(BASIS), diagonal(24 * BASIS)
    for ref in tmps:
        ref[...] = jnp.zeros((128, 128), f32)
    jacobian_weights(jac_ref, tmps[0], w_jac)
    stiff_weights(stiff_ref, -1.0, tmps[1], expand20, diag20, w_stiff_h, w_stiff_l)
    project_weights(proj_ref, tmps[2], expand20, diag20, w_proj, w_proj3)
    w_expand[...] = expand20

    zeros5 = jnp.zeros((5, WIDE), f32)

    def columns(h):
        return slice(h * WIDE, h * WIDE + WIDE)

    def geometry(h):
        return [
            [jnp.broadcast_to(geo_ref[d, j : j + 1, columns(h)], (8, WIDE))[None] for j in range(3)]
            for d in range(3)
        ]

    fine = cluster_ref[...] == 0
    for degree in range(ORDER):
        base = TIME_STEP ** (degree + 1) / math.factorial(degree + 1)
        coarse = base * (2.0 ** (degree + 1) - 1.0)
        times[degree] = jnp.broadcast_to(jnp.where(fine, f32(base), f32(coarse)), (8, ELEM))

    state_copy.wait()
    for h in halves:
        for b in range(BASIS):
            value = jnp.concatenate([state_ref[b, :, columns(h)], zeros5], axis=0)
            fields[h][b] = value
            integrals[h][b] = (times[0, :, columns(h)][None] * value.reshape(4, 8, WIDE)).reshape(32, WIDE)

    def predict(degree, carry):
        phases = [mix_steps(lambda b, h=h: fields[h][b], geometry(h), w_jac, mixes[h]) for h in halves]
        for h in halves:

            def store(s, value, h=h):
                value = value.reshape(BASIS, 8, WIDE)
                rows = slice(8 * s, 8 * s + 8)
                fields[h][:, rows, :] = value
                integrals[h][:, rows, :] += times[degree, :, columns(h)][None] * value

            phases.append(stiff_steps(mixes[h], w_stiff_h, w_stiff_l, store))
        run(*phases)
        return carry

    lax.fori_loop(1, ORDER, predict, 0)

    def operand(h, s):
        high, low = split(integrals[h][:, 8 * s : 8 * s + 8, :].reshape(BASIS * 8, WIDE))
        return jnp.concatenate([high, low, high], axis=0)

    def keep_own(f, h, s, rows):
        own[f, :, 8 * s : 8 * s + 8, columns(h)] = rows.reshape(FACE, 8, WIDE)

    for h in halves:
        operands = [operand(h, s) for s in range(4)]
        packed = dot(w_proj3[...], operands[3])
        for pair in (0, 2):
            slabs = [dot(w_proj[80 * pair : 80 * pair + 160], operands[s]) for s in range(3)]
            for f in (pair, pair + 1):
                pieces = [slab[80 * (f - pair) : 80 * (f - pair) + 80] for slab in slabs]
                for s in range(3):
                    keep_own(f, h, s, pieces[s])
                whole = jnp.concatenate(pieces + [packed[32 * f : 32 * f + 32]], axis=0)
                for t in range(WIDE // 128):
                    base = ROWS * (f * ELEM + h * WIDE + 128 * t)
                    for c in range(ROWS):
                        chunk = whole[128 * c : min(128 * c + 128, TRACE), 128 * t : 128 * t + 128]
                        if c == ROWS - 1:
                            short = jnp.zeros((128 - chunk.shape[0], 128), f32)
                            chunk = jnp.concatenate([chunk, short], axis=0)
                        pool[pl.ds(base + c, 128, stride=ROWS), :] = chunk.T

    for copy in index_copies:
        copy.wait()
    if remote:
        pl.semaphore_wait(barrier, greeted)

    def link(at):
        axis, step = LINKS[at][:2]
        source, goal = (ref.at[pl.ds(PARCEL * at, PARCEL), :] for ref in (ship, arrive))
        if not remote:
            return pltpu.make_async_copy(source, goal, send_sem.at[at])
        return pltpu.make_async_remote_copy(
            src_ref=source,
            dst_ref=goal,
            send_sem=send_sem.at[at],
            recv_sem=recv_sem.at[at],
            device_id={axis: sides[axis, step][1]},
            device_id_type=MESH,
        )

    for at, (axis, step, first, land) in enumerate(LINKS):
        side = 0 if step < 0 else 1
        lane = LANES[axis] + first - STARTS[axis] - side * WIDTHS[axis]
        for n in range(LINK):
            rows = pool[pl.ds(exp_s[side, lane + n], ROWS), :]
            ship[pl.ds(PARCEL * at + 2 * n, 2), :] = rows[0:2]
            thirds[pl.ds(LINK * at + n, 1), :] = rows[2:3]
        packed = thirds[LINK * at : LINK * at + 16, :]
        for k in range(1, 8):
            packed = packed + pltpu.roll(thirds[LINK * at + 16 * k : LINK * at + 16 * k + 16, :], 16 * k, 1)
        ship[PARCEL * at + 2 * LINK : PARCEL * (at + 1), :] = packed
        if remote:
            pl.when(sides[axis, step][0])(link(at).start)
        else:
            link(at).start()

    def unpack(at):
        base = ROWS * (4 * ELEM + LINKS[at][3])
        for c in range(2):
            pool[pl.ds(base + c, LINK, stride=ROWS), :] = arrive[pl.ds(PARCEL * at + c, LINK, stride=2), :]
        packed = arrive[PARCEL * at + 2 * LINK : PARCEL * (at + 1), :]
        for k in range(8):
            rows = packed if k == 0 else pltpu.roll(packed, 128 - 16 * k, 1)
            pool[pl.ds(base + ROWS * 16 * k + 2, 16, stride=ROWS), :] = rows

    for h in halves:
        rows = dot(w_proj[...], operand(h, 3))
        for f in range(4):
            keep_own(f, h, 3, rows[80 * f : 80 * f + 80])
    stiff_weights(vol_ref, 1.0, tmps[3], w_expand[...], diag20, w_vol_h, w_vol_l)
    expand10, diag10 = expander(FACE), diagonal(24 * FACE)
    rotate_weights(rot_ref, tmps[4], expand10, diag10, w_rot, w_rot3)
    lift_weights(lift_ref, tmps[6], tmps[5], expand10, diag10, w_lift)

    phases = [mix_steps(lambda b, h=h: integrals[h][b], geometry(h), w_jac, mixes[h]) for h in halves]
    for h in halves:

        def store(s, value, h=h):
            total[s, :, columns(h)] = value

        phases.append(stiff_steps(mixes[h], w_vol_h, w_vol_l, store))
    run(*phases)

    for at, (axis, step, *_) in enumerate(LINKS):
        if remote:
            @pl.when(sides[axis, -step][0])
            def _(at=at):
                link(at).wait_recv()
                unpack(at)

        else:
            link(at).wait()
            unpack(at)
    if remote:
        for at, (axis, step, *_) in enumerate(LINKS):
            pl.when(sides[axis, step][0])(link(at).wait_send)

    def fetch(f, first, count):
        for n in range(first, first + count):
            near[pl.ds(ROWS * n, ROWS), :] = pool[pl.ds(cols_s[f, n // 128, n % 128], ROWS), :]

    def turned(f, h):
        tiles = []
        for t in range(WIDE // 128):
            base = ROWS * (h * WIDE + 128 * t)
            parts = [near[pl.ds(base + c, 128, stride=ROWS), :].T for c in range(ROWS)]
            tiles.append(jnp.concatenate([parts[0], parts[1], parts[2][: TRACE - 256]], axis=0))
        high, low = split(jnp.concatenate(tiles, axis=1))
        turn = jnp.broadcast_to(orient_ref[f : f + 1, columns(h)], (8, WIDE))[None]
        slabs = []
        for s in range(4):
            rows = slice(80 * s, min(80 * s + 80, TRACE))
            operand = jnp.concatenate([high[rows], low[rows], high[rows]], axis=0)
            ways = dot(w_rot[...] if s < 3 else w_rot3[...], operand).reshape(3, FACE, 8, WIDE)
            slabs.append(jnp.where(turn == 0, ways[0], jnp.where(turn == 1, ways[1], ways[2])))
        return slabs

    def fluxes(f, h, slabs):
        normal = [
            0.5 * jnp.broadcast_to(nrm_ref[j, f : f + 1, columns(h)], (8, WIDE))[None] for j in range(3)
        ]
        speed = 0.5 * jnp.broadcast_to(speed_ref[:, columns(h)], (8, WIDE))[None]
        flux = []
        for i in range(FACE):
            there = jnp.stack([slabs[s][i] for s in range(4)])
            here = own[f, i, :, columns(h)].reshape(4, 8, WIDE)
            high, low = split((here + there).reshape(32, WIDE))
            moved = dot(w_jac[...], jnp.concatenate([high, low, high], axis=0))
            value = speed * (here - there)
            for j in range(3):
                value = value + normal[j] * moved[32 * j : 32 * j + 32].reshape(4, 8, WIDE)
            flux.append(value)
        return flux

    def lifted(f, h, flux):
        for s in range(4):
            high, low = split(jnp.concatenate([flux[i][s] for i in range(FACE)], axis=0))
            operand = jnp.concatenate([high, low, high], axis=0)
            total[s, :, columns(h)] += dot(w_lift[f], operand)

    fetch(0, 0, ELEM)
    slabs = [turned(0, h) for h in halves]
    fetch(1, 0, ELEM)
    for f in range(4):
        flux, later = [], []
        for h in halves:
            if f < 3:
                later.append(turned(f + 1, h))
            flux.append(fluxes(f, h, slabs[h]))
        for h in halves:
            lifted(f, h, flux[h])
            if f < 2:
                fetch(f + 2, h * (ELEM // 2), ELEM // 2)
        slabs = later

    for h in halves:
        keep = jnp.broadcast_to(cluster_ref[:, columns(h)], (8, WIDE)) == 0
        for b in range(BASIS):
            for s in range(4):
                n = min(8, QUANT - 8 * s)
                update = jnp.where(keep, total[s, 8 * b : 8 * b + 8, columns(h)], 0.0)[:n]
                out_ref[b, 8 * s : 8 * s + n, columns(h)] = (
                    state_ref[b, 8 * s : 8 * s + n, columns(h)] + update
                )


def update_call(remote, *args):
    vmem = pl.BlockSpec(memory_space=pltpu.VMEM)
    return pl.pallas_call(
        functools.partial(kernel, remote),
        out_shape=pltpu.VMEM((BASIS, QUANT, ELEM), f32),
        in_specs=[pl.BlockSpec(memory_space=pl.ANY)] + [vmem] * 16,
        out_specs=vmem,
        scratch_shapes=[
            pltpu.VMEM((BASIS, QUANT, ELEM), f32),
            pltpu.VMEM((BASIS, 32, WIDE), f32),
            pltpu.VMEM((BASIS, 32, WIDE), f32),
            pltpu.VMEM((BASIS, 32, WIDE), f32),
            pltpu.VMEM((BASIS, 32, WIDE), f32),
            pltpu.VMEM((4, 960, WIDE), bf16),
            pltpu.VMEM((4, 960, WIDE), bf16),
            pltpu.VMEM((ORDER, 8, ELEM), f32),
            pltpu.VMEM((4, FACE, 32, ELEM), f32),
            pltpu.VMEM((4, 160, ELEM), f32),
            pltpu.VMEM((ROWS * 6 * ELEM, 128), f32),
            pltpu.VMEM((PARCEL * len(LINKS), 128), f32),
            pltpu.VMEM((LINK * len(LINKS), 128), f32),
            pltpu.VMEM((PARCEL * len(LINKS), 128), f32),
            pltpu.VMEM((ROWS * ELEM, 128), f32),
            pltpu.VMEM((4, 4, 128), i32),
            pltpu.SMEM((4, 4, 128), i32),
            pltpu.VMEM((2, ELEM), i32),
            pltpu.SMEM((2, ELEM), i32),
            *[pltpu.VMEM((128, 128), f32)] * 7,
            pltpu.VMEM((96, 480), bf16),
            pltpu.VMEM((96, 96), bf16),
            pltpu.VMEM((160, 480), bf16),
            pltpu.VMEM((160, 480), bf16),
            pltpu.VMEM((160, 480), bf16),
            pltpu.VMEM((160, 480), bf16),
            pltpu.VMEM((320, 480), bf16),
            pltpu.VMEM((128, 480), bf16),
            pltpu.VMEM((240, 240), bf16),
            pltpu.VMEM((240, 96), bf16),
            pltpu.VMEM((4, 160, 240), bf16),
            pltpu.SemaphoreType.DMA((3,)),
            pltpu.SemaphoreType.DMA((8,)),
            pltpu.SemaphoreType.DMA((8,)),
        ],
        compiler_params=pltpu.CompilerParams(
            vmem_limit_bytes=56 * 2**20,
            **(dict(collective_id=0, has_side_effects=True) if remote else {}),
        ),
    )(*args)


def arranged(args):
    state, geometry, normals, speed, cluster, *rest, proj, lift, rot = args
    return (
        state,
        geometry,
        jnp.transpose(normals, (1, 0, 2)),
        speed.reshape(1, ELEM),
        cluster.reshape(1, ELEM),
        *rest,
        jnp.transpose(proj, (1, 0, 2)),
        jnp.transpose(lift, (2, 0, 1)),
        jnp.transpose(rot, (1, 0, 2)),
    )


def per_device(*args):
    return update_call(True, *arranged(args))


def solution(mesh):
    whole = ("strike", "dip", "depth")
    placed = (
        (P(None, None, whole),) * 3 + (P(whole),) * 2 + (P(None, whole),) * 6 + (P(),) * 6
    )
    return jax.shard_map(
        per_device,
        mesh=mesh,
        in_specs=placed,
        out_specs=P(None, None, whole),
        check_vma=False,
    )
```

```python
import functools
import math

import jax
import jax.numpy as jnp
from jax import lax
from jax.experimental import pallas as pl
from jax.experimental.pallas import tpu as pltpu
from jax.sharding import PartitionSpec as P

MESH = pl.DeviceIdType.MESH
BASIS, QUANT, FACE = 20, 27, 10
ELEM = 512
TIME_STEP = 0.5
ORDER = 4
WIDE = 256
ROWS = 3
TRACE = 272
LINK = 128
PARCEL = 2 * LINK + LINK // 8
f32, bf16, i32 = jnp.float32, jnp.bfloat16, jnp.int32

LINKS = (
    ("strike", -1, 0, 256),
    ("strike", 1, 256, 0),
    ("dip", -1, 512, 640),
    ("dip", 1, 640, 512),
    ("depth", -1, 768, 896),
    ("depth", 1, 896, 768),
    ("strike", -1, 128, 384),
    ("strike", 1, 384, 128),
)
LANES = {"strike": 0, "dip": 256, "depth": 384}
STARTS = {"strike": 0, "dip": 512, "depth": 768}
WIDTHS = {"strike": 256, "dip": 128, "depth": 128}


def dot(a, b):
    return jnp.dot(a, b, preferred_element_type=f32)


def split(x):
    high = x.astype(bf16)
    return high, (x - high.astype(f32)).astype(bf16)


def rep8(m):
    n, k = m.shape
    return jnp.broadcast_to(m[:, None, :], (n, 8, k)).reshape(n * 8, k)


def iota(shape, dim):
    return lax.broadcasted_iota(i32, shape, dim)


def ones_where(mask):
    return jnp.where(mask, 1.0, 0.0).astype(bf16)


def expander(count):
    shape = (96, 24 * count)
    row, entry = iota(shape, 0), iota(shape, 1) >> 3
    part = row >> 5
    inner = row & 31
    return ones_where((inner < count) & (entry == part * count + inner))


def diagonal(width):
    return (iota((8, width), 0) == (iota((8, width), 1) & 7))[None]


def kron8(rows, expand, diag):
    n, width = rows.shape[0], expand.shape[1]
    wide = dot(rep8(rows).astype(bf16), expand).reshape(n, 8, width)
    return jnp.where(diag, wide, 0.0).reshape(n * 8, width).astype(bf16)


def lay(tmp_ref, at, m):
    n, k = m.shape
    high, low = (piece.astype(f32) for piece in split(m))
    for part, piece in enumerate((high, high, low)):
        tmp_ref[at : at + n, 32 * part : 32 * part + k] = piece


def third(x):
    return (x * 171) >> 9


def jacobian_weights(jac_ref, tmp_ref, out_ref):
    for j in range(3):
        high, low = split(jac_ref[j])
        at = slice(32 * j, 32 * j + QUANT)
        tmp_ref[0:QUANT, at] = high.astype(f32)
        tmp_ref[32 : 32 + QUANT, at] = high.astype(f32)
        tmp_ref[64 : 64 + QUANT, at] = low.astype(f32)
    out_ref[...] = tmp_ref[...].T[:96, :96].astype(bf16)


def stiff_weights(mat_ref, sign, tmp_ref, expand, diag, high_ref, low_ref):
    for d in range(3):
        high, low = split(sign * mat_ref[d])
        tmp_ref[0:BASIS, 32 * d : 32 * d + BASIS] = high.astype(f32)
        tmp_ref[24 : 24 + BASIS, 32 * d : 32 * d + BASIS] = low.astype(f32)
    high_ref[...] = kron8(tmp_ref[0:BASIS, 0:96], expand, diag)
    low_ref[...] = kron8(tmp_ref[24 : 24 + BASIS, 0:96], expand, diag)


def project_weights(proj_ref, tmp_ref, expand, diag, out_ref, packed_ref):
    for f in range(4):
        lay(tmp_ref, 16 * f, proj_ref[:, f, :])
    for f in range(4):
        out_ref[80 * f : 80 * f + 80] = kron8(tmp_ref[16 * f : 16 * f + FACE, 0:96], expand, diag)
    row = iota((128, 64), 0)
    inner = row & 31
    pick = ones_where((inner < 30) & ((row >> 5) * 16 + third(inner) == iota((128, 64), 1)))
    rows = dot(pick, tmp_ref[0:64, 0:96].astype(bf16)).astype(bf16)
    inner = iota((128, 480), 0) & 31
    same = inner - 3 * third(inner) == (iota((128, 480), 1) & 7)
    packed_ref[...] = jnp.where(same, dot(rows, expand), 0.0).astype(bf16)


def rotate_weights(rot_ref, tmp_ref, expand, diag, out_ref, packed_ref):
    for o in range(3):
        lay(tmp_ref, 16 * o, rot_ref[:, o, :])
    row, col = iota((96, 96), 0), iota((96, 96), 1)
    inner = col & 31
    packed = ones_where((inner < 30) & (row >> 5 == col >> 5) & ((row & 31) == third(inner)))
    inner = iota((8, 96), 1) & 31
    same = (inner - 3 * third(inner) == iota((8, 96), 0))[None]
    for o in range(3):
        rows = tmp_ref[16 * o : 16 * o + FACE, 0:96]
        out_ref[80 * o : 80 * o + 80] = kron8(rows, expand, diag)
        packed_ref[80 * o : 80 * o + 80] = kron8(rows, packed, same)


def lift_weights(lift_ref, turn_ref, tmp_ref, expand, diag, out_ref):
    turn_ref[...] = jnp.zeros((128, 128), f32)
    for f in range(4):
        turn_ref[16 * f : 16 * f + FACE, 0:BASIS] = lift_ref[:, f, :]
    lifts = turn_ref[...].T
    for f in range(4):
        lay(tmp_ref, 24 * f, -lifts[0:BASIS, 16 * f : 16 * f + FACE])
    for f in range(4):
        out_ref[f] = kron8(tmp_ref[24 * f : 24 * f + BASIS, 0:96], expand, diag)


def mixed(field, geo, weights):
    high, low = split(field)
    moved = dot(weights, jnp.concatenate([high, low, high], axis=0))
    n = field.shape[1]
    parts = [moved[32 * j : 32 * j + 32].reshape(4, 8, n) for j in range(3)]
    return [
        (geo[d][0] * parts[0] + geo[d][1] * parts[1] + geo[d][2] * parts[2]).reshape(32, n)
        for d in range(3)
    ]


def mix_steps(load, geo, jac_ref, mix_ref):
    def step(b):
        first, second = (mixed(load(b + i), geo, jac_ref[...]) for i in range(2))
        for d in range(3):
            for s in range(4):
                rows = slice(8 * s, 8 * s + 8)
                high, low = split(jnp.concatenate([first[d][rows], second[d][rows]], axis=0))
                at = (d * BASIS + b) * 8
                mix_ref[s, at : at + 16, :] = high
                mix_ref[s, 480 + at : 480 + at + 16, :] = low

    return [functools.partial(step, b) for b in range(0, BASIS, 2)]


def stiff_steps(mix_ref, weights_ref, low_ref, store):
    def step(s):
        high, low = mix_ref[s, :480], mix_ref[s, 480:]
        store(s, dot(weights_ref[...], high) + dot(weights_ref[...], low) + dot(low_ref[...], high))

    return [functools.partial(step, s) for s in range(4)]


def run(*phases):
    for phase in phases:
        for step in phase:
            step()


def kernel(
    remote,
    state_hbm,
    geo_ref,
    nrm_ref,
    speed_ref,
    cluster_ref,
    nbi_ref,
    nbf_ref,
    orient_ref,
    exs_ref,
    exd_ref,
    exz_ref,
    stiff_ref,
    vol_ref,
    jac_ref,
    proj_ref,
    lift_ref,
    rot_ref,
    out_ref,
    state_ref,
    field_a,
    field_b,
    integral_a,
    integral_b,
    mix_a,
    mix_b,
    times,
    own,
    total,
    pool,
    ship,
    taken,
    arrive,
    near,
    cols_v,
    cols_s,
    exp_v,
    exp_s,
    t0,
    t1,
    t2,
    t3,
    t4,
    t5,
    t6,
    w_expand,
    w_jac,
    w_stiff_h,
    w_stiff_l,
    w_vol_h,
    w_vol_l,
    w_proj,
    w_proj3,
    w_rot,
    w_rot3,
    w_lift,
    cols_sem,
    send_sem,
    recv_sem,
):
    fields, integrals, mixes = (field_a, field_b), (integral_a, integral_b), (mix_a, mix_b)
    tmps = (t0, t1, t2, t3, t4, t5, t6)
    halves = range(ELEM // WIDE)

    sides = {}
    for axis in ("strike", "dip", "depth"):
        for step in (-1, 1):
            if remote:
                pos, count = lax.axis_index(axis), lax.axis_size(axis)
                there = pos > 0 if step < 0 else pos < count - 1
                sides[axis, step] = there, jnp.clip(pos + step, 0, count - 1)
            else:
                sides[axis, step] = True, None

    if remote:
        barrier = pltpu.get_barrier_semaphore()
        greeted = 0
        for (axis, step), (there, target) in sides.items():

            @pl.when(there)
            def _(axis=axis, target=target):
                pl.semaphore_signal(barrier, inc=1, device_id={axis: target}, device_id_type=MESH)

            greeted = greeted + there.astype(i32)

    state_copy = pltpu.make_async_copy(state_hbm, state_ref, cols_sem.at[2])
    state_copy.start()

    index = nbi_ref[...]
    slots = ROWS * jnp.where(index < ELEM, nbf_ref[...] * ELEM + index, 3 * ELEM + index)
    for t in range(ELEM // 128):
        cols_v[:, t, :] = slots[:, 128 * t : 128 * t + 128]
    exp_v[:, 0:256] = ROWS * exs_ref[...]
    exp_v[:, 256:384] = ROWS * exd_ref[...]
    exp_v[:, 384:512] = ROWS * exz_ref[...]
    index_copies = [
        pltpu.make_async_copy(cols_v, cols_s, cols_sem.at[0]),
        pltpu.make_async_copy(exp_v, exp_s, cols_sem.at[1]),
    ]
    for copy in index_copies:
        copy.start()

    expand20, diag20 = expander(BASIS), diagonal(24 * BASIS)
    for ref in tmps:
        ref[...] = jnp.zeros((128, 128), f32)
    jacobian_weights(jac_ref, tmps[0], w_jac)
    stiff_weights(stiff_ref, -1.0, tmps[1], expand20, diag20, w_stiff_h, w_stiff_l)
    project_weights(proj_ref, tmps[2], expand20, diag20, w_proj, w_proj3)
    w_expand[...] = expand20

    zeros5 = jnp.zeros((5, WIDE), f32)

    def columns(h):
        return slice(h * WIDE, h * WIDE + WIDE)

    def geometry(h):
        return [
            [jnp.broadcast_to(geo_ref[d, j : j + 1, columns(h)], (8, WIDE))[None] for j in range(3)]
            for d in range(3)
        ]

    fine = cluster_ref[...] == 0
    for degree in range(ORDER):
        base = TIME_STEP ** (degree + 1) / math.factorial(degree + 1)
        coarse = base * (2.0 ** (degree + 1) - 1.0)
        times[degree] = jnp.broadcast_to(jnp.where(fine, f32(base), f32(coarse)), (8, ELEM))

    state_copy.wait()
    for h in halves:
        for b in range(BASIS):
            value = jnp.concatenate([state_ref[b, :, columns(h)], zeros5], axis=0)
            fields[h][b] = value
            integrals[h][b] = (times[0, :, columns(h)][None] * value.reshape(4, 8, WIDE)).reshape(32, WIDE)

    def predict(degree, carry):
        phases = [mix_steps(lambda b, h=h: fields[h][b], geometry(h), w_jac, mixes[h]) for h in halves]
        for h in halves:

            def store(s, value, h=h):
                value = value.reshape(BASIS, 8, WIDE)
                rows = slice(8 * s, 8 * s + 8)
                fields[h][:, rows, :] = value
                integrals[h][:, rows, :] += times[degree, :, columns(h)][None] * value

            phases.append(stiff_steps(mixes[h], w_stiff_h, w_stiff_l, store))
        run(*phases)
        return carry

    lax.fori_loop(1, ORDER, predict, 0)

    def operand(h, s):
        high, low = split(integrals[h][:, 8 * s : 8 * s + 8, :].reshape(BASIS * 8, WIDE))
        return jnp.concatenate([high, low, high], axis=0)

    def keep_own(f, h, s, rows):
        own[f, :, 8 * s : 8 * s + 8, columns(h)] = rows.reshape(FACE, 8, WIDE)

    for h in halves:
        operands = [operand(h, s) for s in range(4)]
        packed = dot(w_proj3[...], operands[3])
        for pair in (0, 2):
            slabs = [dot(w_proj[80 * pair : 80 * pair + 160], operands[s]) for s in range(3)]
            for f in (pair, pair + 1):
                pieces = [slab[80 * (f - pair) : 80 * (f - pair) + 80] for slab in slabs]
                for s in range(3):
                    keep_own(f, h, s, pieces[s])
                whole = jnp.concatenate(pieces + [packed[32 * f : 32 * f + 32]], axis=0)
                for t in range(WIDE // 128):
                    base = ROWS * (f * ELEM + h * WIDE + 128 * t)
                    for c in range(ROWS):
                        chunk = whole[128 * c : min(128 * c + 128, TRACE), 128 * t : 128 * t + 128]
                        if c == ROWS - 1:
                            short = jnp.zeros((128 - chunk.shape[0], 128), f32)
                            chunk = jnp.concatenate([chunk, short], axis=0)
                        pool[pl.ds(base + c, 128, stride=ROWS), :] = chunk.T

    for copy in index_copies:
        copy.wait()
    if remote:
        pl.semaphore_wait(barrier, greeted)

    def link(at):
        axis, step = LINKS[at][:2]
        source, goal = (ref.at[pl.ds(PARCEL * at, PARCEL), :] for ref in (ship, arrive))
        if not remote:
            return pltpu.make_async_copy(source, goal, send_sem.at[at])
        return pltpu.make_async_remote_copy(
            src_ref=source,
            dst_ref=goal,
            send_sem=send_sem.at[at],
            recv_sem=recv_sem.at[at],
            device_id={axis: sides[axis, step][1]},
            device_id_type=MESH,
        )

    for at, (axis, step, first, land) in enumerate(LINKS):
        side = 0 if step < 0 else 1
        lane = LANES[axis] + first - STARTS[axis] - side * WIDTHS[axis]
        for n in range(LINK):
            taken[pl.ds(ROWS * (LINK * at + n), ROWS), :] = pool[pl.ds(exp_s[side, lane + n], ROWS), :]
        base = ROWS * LINK * at
        for c in range(2):
            ship[PARCEL * at + c * LINK : PARCEL * at + (c + 1) * LINK, :] = taken[
                pl.ds(base + c, LINK, stride=ROWS), :
            ]
        packed = taken[pl.ds(base + 2, 16, stride=ROWS), :]
        for k in range(1, 8):
            packed = packed + pltpu.roll(taken[pl.ds(base + ROWS * 16 * k + 2, 16, stride=ROWS), :], 16 * k, 1)
        ship[PARCEL * at + 2 * LINK : PARCEL * (at + 1), :] = packed
        if remote:
            pl.when(sides[axis, step][0])(link(at).start)
        else:
            link(at).start()

    def unpack(at):
        base = ROWS * (4 * ELEM + LINKS[at][3])
        for c in range(2):
            pool[pl.ds(base + c, LINK, stride=ROWS), :] = arrive[
                PARCEL * at + c * LINK : PARCEL * at + (c + 1) * LINK, :
            ]
        packed = arrive[PARCEL * at + 2 * LINK : PARCEL * (at + 1), :]
        for k in range(8):
            rows = packed if k == 0 else pltpu.roll(packed, 128 - 16 * k, 1)
            pool[pl.ds(base + ROWS * 16 * k + 2, 16, stride=ROWS), :] = rows

    for h in halves:
        rows = dot(w_proj[...], operand(h, 3))
        for f in range(4):
            keep_own(f, h, 3, rows[80 * f : 80 * f + 80])
    stiff_weights(vol_ref, 1.0, tmps[3], w_expand[...], diag20, w_vol_h, w_vol_l)
    expand10, diag10 = expander(FACE), diagonal(24 * FACE)
    rotate_weights(rot_ref, tmps[4], expand10, diag10, w_rot, w_rot3)
    lift_weights(lift_ref, tmps[6], tmps[5], expand10, diag10, w_lift)

    phases = [mix_steps(lambda b, h=h: integrals[h][b], geometry(h), w_jac, mixes[h]) for h in halves]
    for h in halves:

        def store(s, value, h=h):
            total[s, :, columns(h)] = value

        phases.append(stiff_steps(mixes[h], w_vol_h, w_vol_l, store))
    run(*phases)

    for at, (axis, step, *_) in enumerate(LINKS):
        if remote:
            @pl.when(sides[axis, -step][0])
            def _(at=at):
                link(at).wait_recv()
                unpack(at)

        else:
            link(at).wait()
            unpack(at)
    if remote:
        for at, (axis, step, *_) in enumerate(LINKS):
            pl.when(sides[axis, step][0])(link(at).wait_send)

    def fetch(f, first, count):
        for n in range(first, first + count):
            near[pl.ds(ROWS * n, ROWS), :] = pool[pl.ds(cols_s[f, n // 128, n % 128], ROWS), :]

    def turned(f, h):
        tiles = []
        for t in range(WIDE // 128):
            base = ROWS * (h * WIDE + 128 * t)
            parts = [near[pl.ds(base + c, 128, stride=ROWS), :] for c in range(ROWS)]
            tiles.append(
                jnp.concatenate([parts[0].T, parts[1].T, parts[2][:, : TRACE - 256].T], axis=0)
            )
        high, low = split(jnp.concatenate(tiles, axis=1))
        turn = jnp.broadcast_to(orient_ref[f : f + 1, columns(h)], (8, WIDE))[None]
        slabs = []
        for s in range(4):
            rows = slice(80 * s, min(80 * s + 80, TRACE))
            operand = jnp.concatenate([high[rows], low[rows], high[rows]], axis=0)
            ways = dot(w_rot[...] if s < 3 else w_rot3[...], operand).reshape(3, FACE, 8, WIDE)
            slabs.append(jnp.where(turn == 0, ways[0], jnp.where(turn == 1, ways[1], ways[2])))
        return slabs

    def fluxes(f, h, slabs):
        normal = [
            0.5 * jnp.broadcast_to(nrm_ref[j, f : f + 1, columns(h)], (8, WIDE))[None] for j in range(3)
        ]
        speed = 0.5 * jnp.broadcast_to(speed_ref[:, columns(h)], (8, WIDE))[None]
        flux = []
        for i in range(FACE):
            there = jnp.stack([slabs[s][i] for s in range(4)])
            here = own[f, i, :, columns(h)].reshape(4, 8, WIDE)
            high, low = split((here + there).reshape(32, WIDE))
            moved = dot(w_jac[...], jnp.concatenate([high, low, high], axis=0))
            value = speed * (here - there)
            for j in range(3):
                value = value + normal[j] * moved[32 * j : 32 * j + 32].reshape(4, 8, WIDE)
            flux.append(value)
        return flux

    def lifted(f, h, flux):
        for s in range(4):
            high, low = split(jnp.concatenate([flux[i][s] for i in range(FACE)], axis=0))
            operand = jnp.concatenate([high, low, high], axis=0)
            total[s, :, columns(h)] += dot(w_lift[f], operand)

    fetch(0, 0, ELEM)
    slabs = [turned(0, h) for h in halves]
    fetch(1, 0, ELEM)
    for f in range(4):
        flux, later = [], []
        for h in halves:
            if f < 3:
                later.append(turned(f + 1, h))
            flux.append(fluxes(f, h, slabs[h]))
        for h in halves:
            lifted(f, h, flux[h])
            if f < 2:
                fetch(f + 2, h * (ELEM // 2), ELEM // 2)
        slabs = later

    for h in halves:
        keep = jnp.broadcast_to(cluster_ref[:, columns(h)], (8, WIDE)) == 0
        for b in range(BASIS):
            for s in range(4):
                n = min(8, QUANT - 8 * s)
                update = jnp.where(keep, total[s, 8 * b : 8 * b + 8, columns(h)], 0.0)[:n]
                out_ref[b, 8 * s : 8 * s + n, columns(h)] = (
                    state_ref[b, 8 * s : 8 * s + n, columns(h)] + update
                )


def update_call(remote, *args):
    vmem = pl.BlockSpec(memory_space=pltpu.VMEM)
    return pl.pallas_call(
        functools.partial(kernel, remote),
        out_shape=pltpu.VMEM((BASIS, QUANT, ELEM), f32),
        in_specs=[pl.BlockSpec(memory_space=pl.ANY)] + [vmem] * 16,
        out_specs=vmem,
        scratch_shapes=[
            pltpu.VMEM((BASIS, QUANT, ELEM), f32),
            pltpu.VMEM((BASIS, 32, WIDE), f32),
            pltpu.VMEM((BASIS, 32, WIDE), f32),
            pltpu.VMEM((BASIS, 32, WIDE), f32),
            pltpu.VMEM((BASIS, 32, WIDE), f32),
            pltpu.VMEM((4, 960, WIDE), bf16),
            pltpu.VMEM((4, 960, WIDE), bf16),
            pltpu.VMEM((ORDER, 8, ELEM), f32),
            pltpu.VMEM((4, FACE, 32, ELEM), f32),
            pltpu.VMEM((4, 160, ELEM), f32),
            pltpu.VMEM((ROWS * 6 * ELEM, 128), f32),
            pltpu.VMEM((PARCEL * len(LINKS), 128), f32),
            pltpu.VMEM((ROWS * LINK * len(LINKS), 128), f32),
            pltpu.VMEM((PARCEL * len(LINKS), 128), f32),
            pltpu.VMEM((ROWS * ELEM, 128), f32),
            pltpu.VMEM((4, 4, 128), i32),
            pltpu.SMEM((4, 4, 128), i32),
            pltpu.VMEM((2, ELEM), i32),
            pltpu.SMEM((2, ELEM), i32),
            *[pltpu.VMEM((128, 128), f32)] * 7,
            pltpu.VMEM((96, 480), bf16),
            pltpu.VMEM((96, 96), bf16),
            pltpu.VMEM((160, 480), bf16),
            pltpu.VMEM((160, 480), bf16),
            pltpu.VMEM((160, 480), bf16),
            pltpu.VMEM((160, 480), bf16),
            pltpu.VMEM((320, 480), bf16),
            pltpu.VMEM((128, 480), bf16),
            pltpu.VMEM((240, 240), bf16),
            pltpu.VMEM((240, 96), bf16),
            pltpu.VMEM((4, 160, 240), bf16),
            pltpu.SemaphoreType.DMA((3,)),
            pltpu.SemaphoreType.DMA((8,)),
            pltpu.SemaphoreType.DMA((8,)),
        ],
        compiler_params=pltpu.CompilerParams(
            vmem_limit_bytes=56 * 2**20,
            **(dict(collective_id=0, has_side_effects=True) if remote else {}),
        ),
    )(*args)


def arranged(args):
    state, geometry, normals, speed, cluster, *rest, proj, lift, rot = args
    return (
        state,
        geometry,
        jnp.transpose(normals, (1, 0, 2)),
        speed.reshape(1, ELEM),
        cluster.reshape(1, ELEM),
        *rest,
        jnp.transpose(proj, (1, 0, 2)),
        jnp.transpose(lift, (2, 0, 1)),
        jnp.transpose(rot, (1, 0, 2)),
    )


def per_device(*args):
    return update_call(True, *arranged(args))


def solution(mesh):
    whole = ("strike", "dip", "depth")
    placed = (
        (P(None, None, whole),) * 3 + (P(whole),) * 2 + (P(None, whole),) * 6 + (P(),) * 6
    )
    return jax.shard_map(
        per_device,
        mesh=mesh,
        in_specs=placed,
        out_specs=P(None, None, whole),
        check_vma=False,
    )
```

```python
import functools
import math

import jax
import jax.numpy as jnp
from jax import lax
from jax.experimental import pallas as pl
from jax.experimental.pallas import tpu as pltpu
from jax.sharding import PartitionSpec as P

MESH = pl.DeviceIdType.MESH
BASIS, QUANT, FACE = 20, 27, 10
ELEM = 512
TIME_STEP = 0.5
ORDER = 4
WIDE = 256
ROWS = 3
TRACE = 272
LINK = 128
PARCEL = 2 * LINK + LINK // 8
f32, bf16, i32 = jnp.float32, jnp.bfloat16, jnp.int32

LINKS = (
    ("strike", -1, 0, 256),
    ("strike", 1, 256, 0),
    ("strike", -1, 128, 384),
    ("strike", 1, 384, 128),
    ("dip", -1, 512, 640),
    ("dip", 1, 640, 512),
    ("depth", -1, 768, 896),
    ("depth", 1, 896, 768),
)
LANES = {"strike": 0, "dip": 256, "depth": 384}
STARTS = {"strike": 0, "dip": 512, "depth": 768}
WIDTHS = {"strike": 256, "dip": 128, "depth": 128}


def dot(a, b):
    return jnp.dot(a, b, preferred_element_type=f32)


def split(x):
    high = x.astype(bf16)
    return high, (x - high.astype(f32)).astype(bf16)


def rep8(m):
    n, k = m.shape
    return jnp.broadcast_to(m[:, None, :], (n, 8, k)).reshape(n * 8, k)


def iota(shape, dim):
    return lax.broadcasted_iota(i32, shape, dim)


def ones_where(mask):
    return jnp.where(mask, 1.0, 0.0).astype(bf16)


def expander(count):
    shape = (96, 24 * count)
    row, entry = iota(shape, 0), iota(shape, 1) >> 3
    part = row >> 5
    inner = row & 31
    return ones_where((inner < count) & (entry == part * count + inner))


def diagonal(width):
    return (iota((8, width), 0) == (iota((8, width), 1) & 7))[None]


def kron8(rows, expand, diag):
    n, width = rows.shape[0], expand.shape[1]
    wide = dot(rep8(rows).astype(bf16), expand).reshape(n, 8, width)
    return jnp.where(diag, wide, 0.0).reshape(n * 8, width).astype(bf16)


def lay(tmp_ref, at, m):
    n, k = m.shape
    high, low = (piece.astype(f32) for piece in split(m))
    for part, piece in enumerate((high, high, low)):
        tmp_ref[at : at + n, 32 * part : 32 * part + k] = piece


def third(x):
    return (x * 171) >> 9


def jacobian_weights(jac_ref, tmp_ref, out_ref):
    for j in range(3):
        high, low = split(jac_ref[j])
        at = slice(32 * j, 32 * j + QUANT)
        tmp_ref[0:QUANT, at] = high.astype(f32)
        tmp_ref[32 : 32 + QUANT, at] = high.astype(f32)
        tmp_ref[64 : 64 + QUANT, at] = low.astype(f32)
    out_ref[...] = tmp_ref[...].T[:96, :96].astype(bf16)


def stiff_weights(mat_ref, sign, tmp_ref, expand, diag, high_ref, low_ref):
    for d in range(3):
        high, low = split(sign * mat_ref[d])
        tmp_ref[0:BASIS, 32 * d : 32 * d + BASIS] = high.astype(f32)
        tmp_ref[24 : 24 + BASIS, 32 * d : 32 * d + BASIS] = low.astype(f32)
    high_ref[...] = kron8(tmp_ref[0:BASIS, 0:96], expand, diag)
    low_ref[...] = kron8(tmp_ref[24 : 24 + BASIS, 0:96], expand, diag)


def project_weights(proj_ref, tmp_ref, expand, diag, out_ref, packed_ref):
    for f in range(4):
        lay(tmp_ref, 16 * f, proj_ref[:, f, :])
    for f in range(4):
        out_ref[80 * f : 80 * f + 80] = kron8(tmp_ref[16 * f : 16 * f + FACE, 0:96], expand, diag)
    row = iota((128, 64), 0)
    inner = row & 31
    pick = ones_where((inner < 30) & ((row >> 5) * 16 + third(inner) == iota((128, 64), 1)))
    rows = dot(pick, tmp_ref[0:64, 0:96].astype(bf16)).astype(bf16)
    inner = iota((128, 480), 0) & 31
    same = inner - 3 * third(inner) == (iota((128, 480), 1) & 7)
    packed_ref[...] = jnp.where(same, dot(rows, expand), 0.0).astype(bf16)


def rotate_weights(rot_ref, tmp_ref, expand, diag, out_ref, packed_ref):
    for o in range(3):
        lay(tmp_ref, 16 * o, rot_ref[:, o, :])
    row, col = iota((96, 96), 0), iota((96, 96), 1)
    inner = col & 31
    packed = ones_where((inner < 30) & (row >> 5 == col >> 5) & ((row & 31) == third(inner)))
    inner = iota((8, 96), 1) & 31
    same = (inner - 3 * third(inner) == iota((8, 96), 0))[None]
    for o in range(3):
        rows = tmp_ref[16 * o : 16 * o + FACE, 0:96]
        out_ref[80 * o : 80 * o + 80] = kron8(rows, expand, diag)
        packed_ref[80 * o : 80 * o + 80] = kron8(rows, packed, same)


def lift_weights(lift_ref, turn_ref, tmp_ref, expand, diag, out_ref):
    turn_ref[...] = jnp.zeros((128, 128), f32)
    for f in range(4):
        turn_ref[16 * f : 16 * f + FACE, 0:BASIS] = lift_ref[:, f, :]
    lifts = turn_ref[...].T
    for f in range(4):
        lay(tmp_ref, 24 * f, -lifts[0:BASIS, 16 * f : 16 * f + FACE])
    for f in range(4):
        out_ref[f] = kron8(tmp_ref[24 * f : 24 * f + BASIS, 0:96], expand, diag)


def mixed(field, geo, weights):
    high, low = split(field)
    moved = dot(weights, jnp.concatenate([high, low, high], axis=0))
    n = field.shape[1]
    parts = [moved[32 * j : 32 * j + 32].reshape(4, 8, n) for j in range(3)]
    return [
        (geo[d][0] * parts[0] + geo[d][1] * parts[1] + geo[d][2] * parts[2]).reshape(32, n)
        for d in range(3)
    ]


def mix_steps(load, geo, jac_ref, mix_ref):
    def step(b):
        first, second = (mixed(load(b + i), geo, jac_ref[...]) for i in range(2))
        for d in range(3):
            for s in range(4):
                rows = slice(8 * s, 8 * s + 8)
                high, low = split(jnp.concatenate([first[d][rows], second[d][rows]], axis=0))
                at = (d * BASIS + b) * 8
                mix_ref[s, at : at + 16, :] = high
                mix_ref[s, 480 + at : 480 + at + 16, :] = low

    return [functools.partial(step, b) for b in range(0, BASIS, 2)]


def stiff_steps(mix_ref, weights_ref, low_ref, store):
    def step(s):
        high, low = mix_ref[s, :480], mix_ref[s, 480:]
        store(s, dot(weights_ref[...], high) + dot(weights_ref[...], low) + dot(low_ref[...], high))

    return [functools.partial(step, s) for s in range(4)]


def run(*phases):
    for phase in phases:
        for step in phase:
            step()


def kernel(
    remote,
    state_hbm,
    geo_ref,
    nrm_ref,
    speed_ref,
    cluster_ref,
    nbi_ref,
    nbf_ref,
    orient_ref,
    exs_ref,
    exd_ref,
    exz_ref,
    stiff_ref,
    vol_ref,
    jac_ref,
    proj_ref,
    lift_ref,
    rot_ref,
    out_ref,
    state_ref,
    field_a,
    field_b,
    integral_a,
    integral_b,
    mix_a,
    mix_b,
    times,
    own,
    total,
    pool,
    ship,
    taken,
    arrive,
    near,
    cols_v,
    cols_s,
    exp_v,
    exp_s,
    t0,
    t1,
    t2,
    t3,
    t4,
    t5,
    t6,
    w_expand,
    w_jac,
    w_stiff_h,
    w_stiff_l,
    w_vol_h,
    w_vol_l,
    w_proj,
    w_proj3,
    w_rot,
    w_rot3,
    w_lift,
    cols_sem,
    send_sem,
    recv_sem,
):
    fields, integrals, mixes = (field_a, field_b), (integral_a, integral_b), (mix_a, mix_b)
    tmps = (t0, t1, t2, t3, t4, t5, t6)
    halves = range(ELEM // WIDE)

    sides = {}
    for axis in ("strike", "dip", "depth"):
        for step in (-1, 1):
            if remote:
                pos, count = lax.axis_index(axis), lax.axis_size(axis)
                there = pos > 0 if step < 0 else pos < count - 1
                sides[axis, step] = there, jnp.clip(pos + step, 0, count - 1)
            else:
                sides[axis, step] = True, None

    if remote:
        barrier = pltpu.get_barrier_semaphore()
        greeted = 0
        for (axis, step), (there, target) in sides.items():

            @pl.when(there)
            def _(axis=axis, target=target):
                pl.semaphore_signal(barrier, inc=1, device_id={axis: target}, device_id_type=MESH)

            greeted = greeted + there.astype(i32)

    state_copy = pltpu.make_async_copy(state_hbm, state_ref, cols_sem.at[2])
    state_copy.start()

    index = nbi_ref[...]
    slots = ROWS * jnp.where(index < ELEM, nbf_ref[...] * ELEM + index, 3 * ELEM + index)
    for t in range(ELEM // 128):
        cols_v[:, t, :] = slots[:, 128 * t : 128 * t + 128]
    exp_v[:, 0:256] = ROWS * exs_ref[...]
    exp_v[:, 256:384] = ROWS * exd_ref[...]
    exp_v[:, 384:512] = ROWS * exz_ref[...]
    index_copies = [
        pltpu.make_async_copy(cols_v, cols_s, cols_sem.at[0]),
        pltpu.make_async_copy(exp_v, exp_s, cols_sem.at[1]),
    ]
    for copy in index_copies:
        copy.start()

    expand20, diag20 = expander(BASIS), diagonal(24 * BASIS)
    for ref in tmps:
        ref[...] = jnp.zeros((128, 128), f32)
    jacobian_weights(jac_ref, tmps[0], w_jac)
    stiff_weights(stiff_ref, -1.0, tmps[1], expand20, diag20, w_stiff_h, w_stiff_l)
    project_weights(proj_ref, tmps[2], expand20, diag20, w_proj, w_proj3)
    w_expand[...] = expand20

    zeros5 = jnp.zeros((5, WIDE), f32)

    def columns(h):
        return slice(h * WIDE, h * WIDE + WIDE)

    def geometry(h):
        return [
            [jnp.broadcast_to(geo_ref[d, j : j + 1, columns(h)], (8, WIDE))[None] for j in range(3)]
            for d in range(3)
        ]

    fine = cluster_ref[...] == 0
    for degree in range(ORDER):
        base = TIME_STEP ** (degree + 1) / math.factorial(degree + 1)
        coarse = base * (2.0 ** (degree + 1) - 1.0)
        times[degree] = jnp.broadcast_to(jnp.where(fine, f32(base), f32(coarse)), (8, ELEM))

    state_copy.wait()
    for h in halves:
        for b in range(BASIS):
            value = jnp.concatenate([state_ref[b, :, columns(h)], zeros5], axis=0)
            fields[h][b] = value
            integrals[h][b] = (times[0, :, columns(h)][None] * value.reshape(4, 8, WIDE)).reshape(32, WIDE)

    def predict(degree, carry):
        phases = [mix_steps(lambda b, h=h: fields[h][b], geometry(h), w_jac, mixes[h]) for h in halves]
        for h in halves:

            def store(s, value, h=h):
                value = value.reshape(BASIS, 8, WIDE)
                rows = slice(8 * s, 8 * s + 8)
                fields[h][:, rows, :] = value
                integrals[h][:, rows, :] += times[degree, :, columns(h)][None] * value

            phases.append(stiff_steps(mixes[h], w_stiff_h, w_stiff_l, store))
        run(*phases)
        return carry

    lax.fori_loop(1, ORDER, predict, 0)

    def operand(h, s):
        high, low = split(integrals[h][:, 8 * s : 8 * s + 8, :].reshape(BASIS * 8, WIDE))
        return jnp.concatenate([high, low, high], axis=0)

    def keep_own(f, h, s, rows):
        own[f, :, 8 * s : 8 * s + 8, columns(h)] = rows.reshape(FACE, 8, WIDE)

    for h in halves:
        operands = [operand(h, s) for s in range(4)]
        packed = dot(w_proj3[...], operands[3])
        for pair in (0, 2):
            slabs = [dot(w_proj[80 * pair : 80 * pair + 160], operands[s]) for s in range(3)]
            for f in (pair, pair + 1):
                pieces = [slab[80 * (f - pair) : 80 * (f - pair) + 80] for slab in slabs]
                for s in range(3):
                    keep_own(f, h, s, pieces[s])
                whole = jnp.concatenate(pieces + [packed[32 * f : 32 * f + 32]], axis=0)
                for t in range(WIDE // 128):
                    base = ROWS * (f * ELEM + h * WIDE + 128 * t)
                    for c in range(ROWS):
                        chunk = whole[128 * c : min(128 * c + 128, TRACE), 128 * t : 128 * t + 128]
                        if c == ROWS - 1:
                            short = jnp.zeros((128 - chunk.shape[0], 128), f32)
                            chunk = jnp.concatenate([chunk, short], axis=0)
                        pool[pl.ds(base + c, 128, stride=ROWS), :] = chunk.T

    for copy in index_copies:
        copy.wait()
    if remote:
        pl.semaphore_wait(barrier, greeted)

    def link(at):
        axis, step = LINKS[at][:2]
        source, goal = (ref.at[pl.ds(PARCEL * at, PARCEL), :] for ref in (ship, arrive))
        if not remote:
            return pltpu.make_async_copy(source, goal, send_sem.at[at])
        return pltpu.make_async_remote_copy(
            src_ref=source,
            dst_ref=goal,
            send_sem=send_sem.at[at],
            recv_sem=recv_sem.at[at],
            device_id={axis: sides[axis, step][1]},
            device_id_type=MESH,
        )

    for at, (axis, step, first, land) in enumerate(LINKS):
        side = 0 if step < 0 else 1
        lane = LANES[axis] + first - STARTS[axis] - side * WIDTHS[axis]
        for n in range(LINK):
            taken[pl.ds(ROWS * (LINK * at + n), ROWS), :] = pool[pl.ds(exp_s[side, lane + n], ROWS), :]
        base = ROWS * LINK * at
        for c in range(2):
            ship[PARCEL * at + c * LINK : PARCEL * at + (c + 1) * LINK, :] = taken[
                pl.ds(base + c, LINK, stride=ROWS), :
            ]
        packed = taken[pl.ds(base + 2, 16, stride=ROWS), :]
        for k in range(1, 8):
            packed = packed + pltpu.roll(taken[pl.ds(base + ROWS * 16 * k + 2, 16, stride=ROWS), :], 16 * k, 1)
        ship[PARCEL * at + 2 * LINK : PARCEL * (at + 1), :] = packed
        if remote:
            pl.when(sides[axis, step][0])(link(at).start)
        else:
            link(at).start()

    def unpack(at):
        base = ROWS * (4 * ELEM + LINKS[at][3])
        for c in range(2):
            pool[pl.ds(base + c, LINK, stride=ROWS), :] = arrive[
                PARCEL * at + c * LINK : PARCEL * at + (c + 1) * LINK, :
            ]
        packed = arrive[PARCEL * at + 2 * LINK : PARCEL * (at + 1), :]
        for k in range(8):
            rows = packed if k == 0 else pltpu.roll(packed, 128 - 16 * k, 1)
            pool[pl.ds(base + ROWS * 16 * k + 2, 16, stride=ROWS), :] = rows

    for h in halves:
        rows = dot(w_proj[...], operand(h, 3))
        for f in range(4):
            keep_own(f, h, 3, rows[80 * f : 80 * f + 80])
    stiff_weights(vol_ref, 1.0, tmps[3], w_expand[...], diag20, w_vol_h, w_vol_l)
    expand10, diag10 = expander(FACE), diagonal(24 * FACE)
    rotate_weights(rot_ref, tmps[4], expand10, diag10, w_rot, w_rot3)
    lift_weights(lift_ref, tmps[6], tmps[5], expand10, diag10, w_lift)

    phases = [mix_steps(lambda b, h=h: integrals[h][b], geometry(h), w_jac, mixes[h]) for h in halves]
    for h in halves:

        def store(s, value, h=h):
            total[s, :, columns(h)] = value

        phases.append(stiff_steps(mixes[h], w_vol_h, w_vol_l, store))
    run(*phases)

    for at, (axis, step, *_) in enumerate(LINKS):
        if remote:
            @pl.when(sides[axis, -step][0])
            def _(at=at):
                link(at).wait_recv()
                unpack(at)

        else:
            link(at).wait()
            unpack(at)
    if remote:
        for at, (axis, step, *_) in enumerate(LINKS):
            pl.when(sides[axis, step][0])(link(at).wait_send)

    def fetch(f, first, count):
        for n in range(first, first + count):
            near[pl.ds(ROWS * n, ROWS), :] = pool[pl.ds(cols_s[f, n // 128, n % 128], ROWS), :]

    def turned(f, h):
        tiles = []
        for t in range(WIDE // 128):
            base = ROWS * (h * WIDE + 128 * t)
            parts = [near[pl.ds(base + c, 128, stride=ROWS), :] for c in range(ROWS)]
            tiles.append(
                jnp.concatenate([parts[0].T, parts[1].T, parts[2][:, : TRACE - 256].T], axis=0)
            )
        high, low = split(jnp.concatenate(tiles, axis=1))
        turn = jnp.broadcast_to(orient_ref[f : f + 1, columns(h)], (8, WIDE))[None]
        slabs = []
        for s in range(4):
            rows = slice(80 * s, min(80 * s + 80, TRACE))
            operand = jnp.concatenate([high[rows], low[rows], high[rows]], axis=0)
            ways = dot(w_rot[...] if s < 3 else w_rot3[...], operand).reshape(3, FACE, 8, WIDE)
            slabs.append(jnp.where(turn == 0, ways[0], jnp.where(turn == 1, ways[1], ways[2])))
        return slabs

    def fluxes(f, h, slabs):
        normal = [
            0.5 * jnp.broadcast_to(nrm_ref[j, f : f + 1, columns(h)], (8, WIDE))[None] for j in range(3)
        ]
        speed = 0.5 * jnp.broadcast_to(speed_ref[:, columns(h)], (8, WIDE))[None]
        flux = []
        for i in range(FACE):
            there = jnp.stack([slabs[s][i] for s in range(4)])
            here = own[f, i, :, columns(h)].reshape(4, 8, WIDE)
            high, low = split((here + there).reshape(32, WIDE))
            moved = dot(w_jac[...], jnp.concatenate([high, low, high], axis=0))
            value = speed * (here - there)
            for j in range(3):
                value = value + normal[j] * moved[32 * j : 32 * j + 32].reshape(4, 8, WIDE)
            flux.append(value)
        return flux

    def lifted(f, h, flux):
        for s in range(4):
            high, low = split(jnp.concatenate([flux[i][s] for i in range(FACE)], axis=0))
            operand = jnp.concatenate([high, low, high], axis=0)
            total[s, :, columns(h)] += dot(w_lift[f], operand)

    fetch(0, 0, ELEM)
    slabs = [turned(0, h) for h in halves]
    fetch(1, 0, ELEM)
    for f in range(4):
        flux, later = [], []
        for h in halves:
            if f < 3:
                later.append(turned(f + 1, h))
            flux.append(fluxes(f, h, slabs[h]))
        for h in halves:
            lifted(f, h, flux[h])
            if f < 2:
                fetch(f + 2, h * (ELEM // 2), ELEM // 2)
        slabs = later

    for h in halves:
        keep = jnp.broadcast_to(cluster_ref[:, columns(h)], (8, WIDE)) == 0
        for b in range(BASIS):
            for s in range(4):
                n = min(8, QUANT - 8 * s)
                update = jnp.where(keep, total[s, 8 * b : 8 * b + 8, columns(h)], 0.0)[:n]
                out_ref[b, 8 * s : 8 * s + n, columns(h)] = (
                    state_ref[b, 8 * s : 8 * s + n, columns(h)] + update
                )


def update_call(remote, *args):
    vmem = pl.BlockSpec(memory_space=pltpu.VMEM)
    return pl.pallas_call(
        functools.partial(kernel, remote),
        out_shape=pltpu.VMEM((BASIS, QUANT, ELEM), f32),
        in_specs=[pl.BlockSpec(memory_space=pl.ANY)] + [vmem] * 16,
        out_specs=vmem,
        scratch_shapes=[
            pltpu.VMEM((BASIS, QUANT, ELEM), f32),
            pltpu.VMEM((BASIS, 32, WIDE), f32),
            pltpu.VMEM((BASIS, 32, WIDE), f32),
            pltpu.VMEM((BASIS, 32, WIDE), f32),
            pltpu.VMEM((BASIS, 32, WIDE), f32),
            pltpu.VMEM((4, 960, WIDE), bf16),
            pltpu.VMEM((4, 960, WIDE), bf16),
            pltpu.VMEM((ORDER, 8, ELEM), f32),
            pltpu.VMEM((4, FACE, 32, ELEM), f32),
            pltpu.VMEM((4, 160, ELEM), f32),
            pltpu.VMEM((ROWS * 6 * ELEM, 128), f32),
            pltpu.VMEM((PARCEL * len(LINKS), 128), f32),
            pltpu.VMEM((ROWS * LINK * len(LINKS), 128), f32),
            pltpu.VMEM((PARCEL * len(LINKS), 128), f32),
            pltpu.VMEM((ROWS * ELEM, 128), f32),
            pltpu.VMEM((4, 4, 128), i32),
            pltpu.SMEM((4, 4, 128), i32),
            pltpu.VMEM((2, ELEM), i32),
            pltpu.SMEM((2, ELEM), i32),
            *[pltpu.VMEM((128, 128), f32)] * 7,
            pltpu.VMEM((96, 480), bf16),
            pltpu.VMEM((96, 96), bf16),
            pltpu.VMEM((160, 480), bf16),
            pltpu.VMEM((160, 480), bf16),
            pltpu.VMEM((160, 480), bf16),
            pltpu.VMEM((160, 480), bf16),
            pltpu.VMEM((320, 480), bf16),
            pltpu.VMEM((128, 480), bf16),
            pltpu.VMEM((240, 240), bf16),
            pltpu.VMEM((240, 96), bf16),
            pltpu.VMEM((4, 160, 240), bf16),
            pltpu.SemaphoreType.DMA((3,)),
            pltpu.SemaphoreType.DMA((8,)),
            pltpu.SemaphoreType.DMA((8,)),
        ],
        compiler_params=pltpu.CompilerParams(
            vmem_limit_bytes=56 * 2**20,
            **(dict(collective_id=0, has_side_effects=True) if remote else {}),
        ),
    )(*args)


def arranged(args):
    state, geometry, normals, speed, cluster, *rest, proj, lift, rot = args
    return (
        state,
        geometry,
        jnp.transpose(normals, (1, 0, 2)),
        speed.reshape(1, ELEM),
        cluster.reshape(1, ELEM),
        *rest,
        jnp.transpose(proj, (1, 0, 2)),
        jnp.transpose(lift, (2, 0, 1)),
        jnp.transpose(rot, (1, 0, 2)),
    )


def per_device(*args):
    return update_call(True, *arranged(args))


def solution(mesh):
    whole = ("strike", "dip", "depth")
    placed = (
        (P(None, None, whole),) * 3 + (P(whole),) * 2 + (P(None, whole),) * 6 + (P(),) * 6
    )
    return jax.shard_map(
        per_device,
        mesh=mesh,
        in_specs=placed,
        out_specs=P(None, None, whole),
        check_vma=False,
    )
```
